256 devices in a mesh: chan: 32 (over z, x), tm: 8 (over y, core).
Axes of the slice: x: 4, y: 4, z: 8, core: 2. Of those that a mesh axis runs over, the one named last changes fastest.
Arguments:
- solution: float32 [2, 8, 1024, 8192], P(None, None, 'chan', 'tm'), may hold values from -6 to 6
- residual: float32 [2, 8, 1024, 8192], P(None, None, 'chan', 'tm'), may hold values from -80 to 80
- direction: float32 [2, 8, 1024, 8192], P(None, None, 'chan', 'tm'), may hold values from -80 to 80
- sample_weight: float32 [8, 32, 32, 2048], P('tm', 'chan'), may hold values from 0.15 to 3
Outputs:
- new_solution: float32 [2, 8, 1024, 8192], P(None, None, 'chan', 'tm')
- new_residual: float32 [2, 8, 1024, 8192], P(None, None, 'chan', 'tm')
- new_direction: float32 [2, 8, 1024, 8192], P(None, None, 'chan', 'tm')
The draws below stay inside these ranges and needn't reach their ends.
All inputs are finite; a program needn't handle non-finite values.
Results may differ from the reference program's by a relative error of at most 0.00012.
Values sent between devices are 32-bit elements; how exact they have to be, the bound alone decides.
A program may use at most 128 MiB of HBM per device.

```python
import math
import jax
import jax.numpy as jnp
from jax import lax

SAMPLES = 2048
CHANNELS = 1024
TAPS = 4
FEEDS = 8
FRAMES = 8192
SEGMENTS = 8
BLOCKS = 32
BLOCK_LEN = 32


def scaled_field(key, base, chan_power, frame_power):
    chan_key, frame_key = jax.random.split(key)
    chan_pos = jnp.arange(CHANNELS, dtype=jnp.float32) / CHANNELS - 0.5
    frame_pos = jnp.arange(FRAMES, dtype=jnp.float32) / FRAMES - 0.5
    chan_scale = chan_power ** chan_pos * jax.random.uniform(chan_key, (CHANNELS,), jnp.float32, 0.7, 1.4)
    frame_scale = frame_power ** frame_pos * jax.random.uniform(frame_key, (FRAMES,), jnp.float32, 0.7, 1.4)
    return base * chan_scale[:, None] * frame_scale[None, :]


def draw_residual(key, part):
    key = jax.random.fold_in(key, 11)
    base_key, scale_key = jax.random.split(key)
    shape = (2, FEEDS, CHANNELS, FRAMES)
    base = jnp.clip(jax.random.normal(base_key, shape, jnp.float32), -4.0, 4.0)
    return scaled_field(scale_key, base, 10.0, 10.0)


def draw_direction(key, part):
    key = jax.random.fold_in(key, 23)
    base_key, scale_key = jax.random.split(key)
    shape = (2, FEEDS, CHANNELS, FRAMES)
    base = jnp.clip(jax.random.normal(base_key, shape, jnp.float32), -4.0, 4.0)
    return scaled_field(scale_key, base, 10.0, 10.0)


def draw_sample_weight(key, part):
    key = jax.random.fold_in(key, 37)
    shape = (SEGMENTS, BLOCKS, BLOCK_LEN, SAMPLES)
    level = jax.random.uniform(key, shape, jnp.float32, math.log(0.15), math.log(3.0))
    return jnp.clip(jnp.exp(level), 0.15, 3.0)


def block_levels(stream_key, extent, pieces, low, high):
    def one(dim, blocks):
        draws = jax.random.uniform(jax.random.fold_in(jax.random.fold_in(stream_key, 6), dim), (blocks,), jnp.float32, low / len(pieces), high / len(pieces))
        return jnp.repeat(jnp.exp(draws), extent[dim] // blocks).reshape((-1,) + (1,) * (len(extent) - dim - 1))

    gain = one(*pieces[0])
    for cut in pieces[1:]:
        gain = gain * one(*cut)
    return gain


def normal_values(own_key, dims, deviation, reach, pieces=(), held_as=jnp.bfloat16):
    drawn = jax.random.normal(own_key, dims, jnp.float32) * deviation
    if len(pieces) > 0:
        drawn = block_levels(own_key, dims, pieces, -0.22, 0.18) * drawn
    return jnp.clip(drawn, min=-reach, max=reach).astype(held_as)


def setup_inputs(seed: int = 0) -> dict:
    key_list = jax.random.split(jax.random.key(seed), 5)
    return {
        "solution": normal_values(key_list[0], (2, FEEDS, CHANNELS, FRAMES), 1.0, 6.0, ((2, 32), (3, 8)), jnp.float32),
        "residual": draw_residual(jax.random.fold_in(key_list[4], 71), 0),
        "direction": draw_direction(jax.random.fold_in(key_list[4], 71), 0),
        "sample_weight": draw_sample_weight(jax.random.fold_in(key_list[4], 71), 0),
    }


def pfb_window():
    position = jnp.arange(TAPS * SAMPLES, dtype=jnp.float32)
    taper = 0.5 - 0.5 * jnp.cos(2.0 * math.pi * position / (TAPS * SAMPLES - 1))
    return (jnp.sinc(position / SAMPLES - TAPS / 2) * taper).reshape(TAPS, SAMPLES)

def one_feed(spectra, noise):
    scale = math.sqrt(SAMPLES)
    window = pfb_window()
    coeffs = jnp.transpose(spectra[0] + 1j * spectra[1])
    padded = jnp.pad(coeffs, ((0, 0), (0, SAMPLES - CHANNELS)))
    samples = jnp.real(jnp.fft.ifft(padded, axis=-1)) * scale
    adjoint = jnp.zeros_like(samples)
    for tap_index in range(TAPS):
        delayed = jnp.pad(samples, ((tap_index, 0), (0, 0)))[:FRAMES]
        adjoint = adjoint + window[tap_index] * delayed
    stream = noise * adjoint
    weighted = jnp.zeros_like(stream)
    for tap_index in range(TAPS):
        advanced = jnp.pad(stream, ((0, tap_index), (0, 0)))[tap_index:]
        weighted = weighted + window[tap_index] * advanced
    spectrum = jnp.fft.rfft(weighted, axis=-1)[:, :CHANNELS] / scale
    return jnp.stack([jnp.transpose(jnp.real(spectrum)), jnp.transpose(jnp.imag(spectrum))])

def reference(solution, residual, direction, sample_weight):
    noise = sample_weight.reshape(FRAMES, SAMPLES)

    def per_feed(spectra):
        return one_feed(spectra, noise)
    image = jnp.moveaxis(lax.map(per_feed, jnp.moveaxis(direction, 1, 0)), 0, 1)
    norm_now = jnp.sum(residual * residual)
    curvature = jnp.sum(direction * image)
    alpha = norm_now / curvature
    new_solution = solution + alpha * direction
    new_residual = residual - alpha * image
    norm_next = jnp.sum(new_residual * new_residual)
    new_direction = new_residual + norm_next / norm_now * direction
    return (new_solution, new_residual, new_direction)
```

```python
import math

import jax
import jax.numpy as jnp
import ml_dtypes
import numpy as np
from jax import lax
from jax.experimental import pallas as pl
from jax.experimental.pallas import tpu as pltpu
from jax.sharding import PartitionSpec as P

MESH = pl.DeviceIdType.MESH
F32 = jnp.float32
BF16 = jnp.bfloat16

SAMPLES = 2048
CHANNELS = 1024
TAPS = 4
FEEDS = 8
GROUPS = 32
SEGMENTS = 8
BLOCK = 32
KHERE = 32
HALF = 2
ACROSS = 4
LANES = ACROSS * BLOCK
RIM = 64
RADIX = 8
ROWS = SAMPLES // RADIX
QUARTER = 4
GQ = GROUPS // QUARTER
INNER = GQ * 2 * KHERE
ROOT_HALF = math.sqrt(0.5)


def tables():
    j = np.arange(CHANNELS // QUARTER)
    r = np.arange(ROWS)
    s = np.arange(RADIX)
    turns = (j[None, None, :] * (RADIX * r[None, :, None] + s[:, None, None])) % SAMPLES
    angle = 2.0 * np.pi * turns / SAMPLES
    scale = 1.0 / math.sqrt(SAMPLES)
    both = np.stack([np.cos(angle) * scale, -np.sin(angle) * scale], axis=2)
    both = both.reshape(RADIX, ROWS, 2, GQ, KHERE).transpose(0, 1, 3, 2, 4)
    full = both.reshape(RADIX, ROWS, INNER)
    high = full.astype(np.float32).astype(ml_dtypes.bfloat16)
    low = (full - high.astype(np.float64)).astype(np.float32).astype(ml_dtypes.bfloat16)
    forward = np.concatenate([high, low], axis=1)
    backward = np.concatenate([high.transpose(0, 2, 1), low.transpose(0, 2, 1)], axis=1)
    return forward, backward


def window_table():
    position = np.arange(TAPS * SAMPLES, dtype=np.float64)
    taper = 0.5 - 0.5 * np.cos(2.0 * np.pi * position / (TAPS * SAMPLES - 1))
    window = (np.sinc(position / SAMPLES - TAPS / 2) * taper).astype(np.float32)
    window = window.reshape(TAPS, ROWS, RADIX).transpose(0, 2, 1)
    return np.ascontiguousarray(np.broadcast_to(window[..., None], (TAPS, RADIX, ROWS, LANES)))


def copy_to(src, dst, ssem, rsem, device):
    return pltpu.make_async_remote_copy(
        src_ref=src, dst_ref=dst, send_sem=ssem, recv_sem=rsem, device_id=device, device_id_type=MESH
    )


def loop(n, body, init=None):
    if init is None:
        def plain(i, carry):
            body(i)
            return carry

        lax.fori_loop(0, n, plain, 0)
        return None
    return lax.fori_loop(0, n, body, init)


def fold_rows(x):
    rows, cols = x.shape
    total = None
    for i in range(rows // 8):
        for j in range(cols // LANES):
            y = x[8 * i : 8 * i + 8, LANES * j : LANES * (j + 1)]
            total = y if total is None else total + y
    return total


def exchange_kernel(
    sol_hbm, res_hbm, dir_hbm, wgt_hbm, tf_hbm, tb_hbm, win_hbm,
    nsol, nres, dirv, beta_ref,
    recvf, sendb, recvb, down_s, down_r, up_s, up_r,
    tf, tb, win, raw, nat, noise, bx, sm, st, bw, vv,
    part_c, part_t,
    load_sem, self_sem, fs, fr, bs, br, halo_s, halo_r, ns, nr, cs, cr, ts, tr,
):
    c = lax.axis_index("chan")
    t = lax.axis_index("tm")
    z, x_here = c // ACROSS, lax.rem(c, ACROSS)

    up_dev = (lax.rem(c + ACROSS, GROUPS), lax.rem(t + (c + ACROSS) // GROUPS, SEGMENTS))
    down_dev = (
        lax.rem(c + GROUPS - ACROSS, GROUPS),
        lax.rem(t + SEGMENTS - 1 + (c + GROUPS - ACROSS) // GROUPS, SEGMENTS),
    )
    barrier = pltpu.get_barrier_semaphore()

    def greet_chan(i):
        pl.semaphore_signal(
            barrier, inc=1, device_id=(lax.rem(c + i + 1, GROUPS), t), device_id_type=MESH
        )

    def greet_tm(i):
        pl.semaphore_signal(
            barrier, inc=1, device_id=(c, lax.rem(t + i + 1, SEGMENTS)), device_id_type=MESH
        )

    loads = [
        pltpu.make_async_copy(src, dst, load_sem.at[i])
        for i, (src, dst) in enumerate(
            (
                (dir_hbm, dirv),
                (wgt_hbm.at[0, 0], raw.at[x_here]),
                (res_hbm, nres),
                (tf_hbm, tf),
                (win_hbm, win),
                (tb_hbm, tb),
                (sol_hbm, nsol),
            )
        )
    ]
    for cp in loads:
        cp.start()
    loop(GROUPS - 1, greet_chan)
    loop(SEGMENTS - 1, greet_tm)
    pl.semaphore_signal(barrier, inc=1, device_id=up_dev, device_id_type=MESH)
    pl.semaphore_signal(barrier, inc=1, device_id=down_dev, device_id_type=MESH)

    def frames_of(zz):
        return pl.ds(pl.multiple_of(zz * LANES, LANES), LANES)

    def forward_copy(h, i):
        d = lax.rem(c + i + 1, GROUPS)
        src = dirv.at[:, HALF * lax.rem(d, ACROSS) + h, :, frames_of(d // ACROSS)]
        return copy_to(src, recvf.at[h, c], fs.at[h, d], fr.at[h, c], (d, t))

    def forward_arrival(h, i):
        d = lax.rem(c + GROUPS - 1 - i, GROUPS)
        return copy_to(recvf.at[h, d], recvf.at[h, d], fs.at[h, d], fr.at[h, d], (d, t))

    def backward_copy(h, i):
        d = lax.rem(c + i + 1, GROUPS)
        dst = recvb.at[:, HALF * x_here + h, :, frames_of(z)]
        return copy_to(sendb.at[h, d], dst, bs.at[h, d], br.at[h, c], (d, t))

    def backward_arrival(h, i):
        d = lax.rem(c + GROUPS - 1 - i, GROUPS)
        dst = recvb.at[:, HALF * lax.rem(d, ACROSS) + h, :, frames_of(d // ACROSS)]
        return copy_to(sendb.at[h, d], dst, bs.at[h, d], br.at[h, d], (d, t))

    def noise_copy(i):
        xx = lax.rem(x_here + i + 1, ACROSS)
        return copy_to(
            raw.at[x_here], raw.at[x_here], ns.at[xx], nr.at[x_here], (z * ACROSS + xx, t)
        )

    def noise_arrival(i):
        xx = lax.rem(x_here + i + 1, ACROSS)
        return copy_to(raw.at[xx], raw.at[xx], ns.at[xx], nr.at[xx], (z * ACROSS + xx, t))

    here = (HALF * x_here, frames_of(z))
    self_f = [
        pltpu.make_async_copy(dirv.at[:, here[0] + h, :, here[1]], recvf.at[h, c], self_sem.at[0, h])
        for h in range(HALF)
    ]
    self_b = [
        pltpu.make_async_copy(sendb.at[h, c], recvb.at[:, here[0] + h, :, here[1]], self_sem.at[1, h])
        for h in range(HALF)
    ]

    loads[0].wait()
    for h in range(HALF):
        self_f[h].start()
    pl.semaphore_wait(barrier, GROUPS - 1 + SEGMENTS - 1 + 2)
    loop(GROUPS - 1, lambda i: forward_copy(0, i).start())
    loads[1].wait()
    loop(ACROSS - 1, lambda i: noise_copy(i).start())
    loop(GROUPS - 1, lambda i: forward_copy(1, i).start())

    loads[2].wait()

    def square(i, acc):
        part, f = i // FEEDS, lax.rem(i, FEEDS)
        y = nres[part, f]
        return acc + fold_rows(y * y)

    norm_part = loop(2 * FEEDS, square, jnp.zeros((8, LANES), F32))

    loop(ACROSS - 1, lambda i: noise_arrival(i).wait_recv())

    def turn(i):
        cols = pl.ds(pl.multiple_of(i * 128, 128), 128)
        nat[cols, :] = jnp.concatenate([raw[q, :, cols] for q in range(ACROSS)], axis=0).T

    loop(SAMPLES // 128, turn)
    for s in range(RADIX):
        noise[s] = nat[pl.ds(s, ROWS, stride=RADIX), :]
    for cp in loads[3:]:
        cp.wait()

    keep_down = jnp.where((z == 0) & (t == 0), 0.0, 1.0).astype(F32)
    keep_up = jnp.where((z == GROUPS // ACROSS - 1) & (t == SEGMENTS - 1), 0.0, 1.0).astype(F32)

    def split_store(ref, where, x):
        high = x.astype(BF16)
        low = (x - high.astype(F32)).astype(BF16)
        ref[where + (slice(0, LANES),)] = high
        ref[where + (slice(LANES, 2 * LANES),)] = low

    def quadrants(x, rows):
        return (x[:rows, :LANES] + x[:rows, LANES:]) + (x[rows:, :LANES] + x[rows:, LANES:])

    RB = 16
    lane = lax.broadcasted_iota(jnp.int32, (RB, LANES), 1)
    slot = lane // TAPS
    GROUP_ROWS = [(s, q) for s in range(RADIX) for q in range(ROWS // RIM)]

    def rolled(x, by):
        by = by % LANES
        return pltpu.roll(x, by, 1) if by else x

    def fold_in(h):
        def body(g):
            re = [recvf[h, p * GQ + g, 0] for p in range(QUARTER)]
            im = [recvf[h, p * GQ + g, 1] for p in range(QUARTER)]

            def pairs(a, b):
                return [
                    (re[a] + re[b], im[a] + im[b]),
                    (re[a] - im[b], im[a] + re[b]),
                    (re[a] - re[b], im[a] - im[b]),
                    (re[a] + im[b], im[a] - re[b]),
                ]

            u, v = pairs(0, 2), pairs(1, 3)
            w = [
                v[0],
                ((v[1][0] - v[1][1]) * ROOT_HALF, (v[1][0] + v[1][1]) * ROOT_HALF),
                (-v[2][1], v[2][0]),
                (-(v[3][0] + v[3][1]) * ROOT_HALF, (v[3][0] - v[3][1]) * ROOT_HALF),
            ]
            for s in range(4):
                for part in range(2):
                    split_store(bx, (s, g, part, slice(None)), u[s][part] + w[s][part])
                    split_store(bx, (s + 4, g, part, slice(None)), u[s][part] - w[s][part])

        loop(GQ, body)

    def to_samples():
        def body(s):
            x = bx[s].reshape(INNER, 2 * LANES)
            sm[s] = quadrants(jnp.dot(tf[s], x, preferred_element_type=F32), ROWS)

        loop(RADIX, body)

    def pack_down(h):
        def body(i):
            out = jnp.zeros((RB, LANES), F32)
            for n, (s, q) in enumerate(GROUP_ROWS):
                rows = pl.ds(pl.multiple_of(q * RIM + i * RB, RB), RB)
                out = jnp.where(slot == n, rolled(sm[s, rows, :], TAPS * n + TAPS), out)
            down_s[h, pl.ds(pl.multiple_of(i * RB, RB), RB), :] = out

        loop(RIM // RB, body)

    def make_stream(h, acc):
        def body(i, acc):
            packed = pl.ds(pl.multiple_of(i * RB, RB), RB)
            below = down_r[h, packed, :] * keep_down
            out = jnp.zeros((RB, LANES), F32)
            for n, (s, q) in enumerate(GROUP_ROWS):
                rows = pl.ds(pl.multiple_of(q * RIM + i * RB, RB), RB)
                x = sm[s, rows, :]
                rim = rolled(below, -TAPS * n - TAPS)
                total = win[0, s, rows, :] * x
                for k in range(1, TAPS):
                    total = total + win[k, s, rows, :] * rolled(jnp.where(lane >= LANES - k, rim, x), k)
                y = noise[s, rows, :] * total
                st[s, rows, :] = y
                acc = acc + fold_rows(y * total)
                out = jnp.where(slot == n, rolled(y, TAPS * n), out)
            up_s[h, packed, :] = out
            return acc

        return loop(RIM // RB, body, acc)

    def make_weighted(h):
        def body(i):
            packed = pl.ds(pl.multiple_of(i * RB, RB), RB)
            above = up_r[h, packed, :] * keep_up
            for n, (s, q) in enumerate(GROUP_ROWS):
                rows = pl.ds(pl.multiple_of(q * RIM + i * RB, RB), RB)
                x = st[s, rows, :]
                rim = rolled(above, -TAPS * n)
                total = win[0, s, rows, :] * x
                for k in range(1, TAPS):
                    total = total + win[k, s, rows, :] * rolled(jnp.where(lane < k, rim, x), -k)
                split_store(bw, (s, rows), total)

        loop(RIM // RB, body)

    def to_spectra():
        def body(s):
            x = quadrants(jnp.dot(tb[s], bw[s], preferred_element_type=F32), INNER)
            vv[s] = x.reshape(GQ, 2, KHERE, LANES)

        loop(RADIX, body)

    def fold_out(h):
        def body(g):
            re = [vv[s, g, 0] for s in range(RADIX)]
            im = [vv[s, g, 1] for s in range(RADIX)]
            ar = [re[s] + re[s + 4] for s in range(4)]
            ai = [im[s] + im[s + 4] for s in range(4)]
            dr = [re[s] - re[s + 4] for s in range(4)]
            di = [im[s] - im[s + 4] for s in range(4)]
            one = ((dr[1] + di[1]) * ROOT_HALF, (di[1] - dr[1]) * ROOT_HALF)
            one3 = ((di[1] - dr[1]) * ROOT_HALF, -(di[1] + dr[1]) * ROOT_HALF)
            three = ((di[3] - dr[3]) * ROOT_HALF, -(di[3] + dr[3]) * ROOT_HALF)
            three3 = ((dr[3] + di[3]) * ROOT_HALF, (di[3] - dr[3]) * ROOT_HALF)
            image = [
                ((ar[0] + ar[2]) + (ar[1] + ar[3]), (ai[0] + ai[2]) + (ai[1] + ai[3])),
                ((dr[0] + di[2]) + (one[0] + three[0]), (di[0] - dr[2]) + (one[1] + three[1])),
                ((ar[0] - ar[2]) + (ai[1] - ai[3]), (ai[0] - ai[2]) + (ar[3] - ar[1])),
                ((dr[0] - di[2]) + (one3[0] + three3[0]), (di[0] + dr[2]) + (one3[1] + three3[1])),
            ]
            for p in range(QUARTER):
                for part in range(2):
                    sendb[h, p * GQ + g, part] = image[p][part]

        loop(GQ, body)

    def tm_copy(rnd, i):
        d = lax.rem(t + i + 1, SEGMENTS)
        return copy_to(part_t.at[rnd, t], part_t.at[rnd, t], ts.at[rnd, d], tr.at[rnd, t], (c, d))

    def tm_arrival(rnd, i):
        d = lax.rem(t + i + 1, SEGMENTS)
        return copy_to(part_t.at[rnd, d], part_t.at[rnd, d], ts.at[rnd, d], tr.at[rnd, d], (c, d))

    def chan_copy(rnd, i):
        d = lax.rem(c + i + 1, GROUPS)
        return copy_to(part_c.at[rnd, c], part_c.at[rnd, c], cs.at[rnd, d], cr.at[rnd, c], (d, t))

    def chan_arrival(rnd, i):
        d = lax.rem(c + i + 1, GROUPS)
        return copy_to(part_c.at[rnd, d], part_c.at[rnd, d], cs.at[rnd, d], cr.at[rnd, d], (d, t))

    def sum_start(rnd, row):
        part_t[rnd, t] = row
        loop(SEGMENTS - 1, lambda i: tm_copy(rnd, i).start())

    def sum_middle(rnd):
        loop(SEGMENTS - 1, lambda i: tm_arrival(rnd, i).wait_recv())
        part_c[rnd, c] = jnp.sum(part_t[rnd], axis=0)
        loop(GROUPS - 1, lambda i: chan_copy(rnd, i).start())

    def sum_end(rnd):
        loop(GROUPS - 1, lambda i: chan_arrival(rnd, i).wait_recv())
        total = jnp.sum(part_c[rnd], axis=0)
        loop(SEGMENTS - 1, lambda i: tm_copy(rnd, i).wait_send())
        loop(GROUPS - 1, lambda i: chan_copy(rnd, i).wait_send())
        return total

    lane_row = lax.broadcasted_iota(jnp.int32, (1, LANES), 1)

    def both(first, second):
        a = jnp.sum(first, axis=0, keepdims=True)
        b = jnp.sum(second, axis=0, keepdims=True)
        half = LANES // 2
        return jnp.where(lane_row < half, a + pltpu.roll(a, half, 1), b + pltpu.roll(b, half, 1))

    curve = jnp.zeros((8, LANES), F32)
    for h in range(HALF):
        self_f[h].wait()
        loop(GROUPS - 1, lambda i: forward_arrival(h, i).wait_recv())
        fold_in(h)
        to_samples()
        pack_down(h)
        down = copy_to(down_s.at[h], down_r.at[h], halo_s.at[0, h], halo_r.at[0, h], up_dev)
        down.start()
        down.wait_recv()
        curve = make_stream(h, curve)
        up = copy_to(up_s.at[h], up_r.at[h], halo_s.at[1, h], halo_r.at[1, h], down_dev)
        up.start()
        if h == HALF - 1:
            sum_start(0, both(norm_part, curve))
        up.wait_recv()
        make_weighted(h)
        to_spectra()
        fold_out(h)
        if h == HALF - 1:
            sum_middle(0)
        loop(GROUPS - 1, lambda i: backward_copy(h, i).start())
        self_b[h].start()
        down.wait_send()
        up.wait_send()

    sums = sum_end(0)
    zero = jnp.zeros((1, LANES), F32)
    norm_now = jnp.sum(jnp.where(lane_row < LANES // 2, sums, zero), axis=1, keepdims=True)
    alpha = norm_now / jnp.sum(jnp.where(lane_row < LANES // 2, zero, sums), axis=1, keepdims=True)

    def step_solution(i):
        part, f = i // FEEDS, lax.rem(i, FEEDS)
        nsol[part, f] = nsol[part, f] + alpha * dirv[part, f]

    loop(2 * FEEDS, step_solution)

    norm_next = jnp.zeros((8, LANES), F32)
    for h in range(HALF):
        self_b[h].wait()
        loop(GROUPS - 1, lambda i: backward_arrival(h, i).wait_recv())

        def update(i, acc):
            part, f = i // ACROSS, HALF * lax.rem(i, ACROSS) + h
            y = nres[part, f] - alpha * recvb[part, f]
            nres[part, f] = y
            return acc + fold_rows(y * y)

        norm_next = loop(2 * ACROSS, update, norm_next)

    sum_start(1, jnp.sum(norm_next, axis=0, keepdims=True))
    sum_middle(1)
    total = jnp.sum(sum_end(1), axis=1, keepdims=True)
    beta_ref[...] = jnp.broadcast_to(total / norm_now, (8, LANES))
    for h in range(HALF):
        loop(GROUPS - 1, lambda i: forward_copy(h, i).wait_send())
        loop(GROUPS - 1, lambda i: backward_copy(h, i).wait_send())
    loop(ACROSS - 1, lambda i: noise_copy(i).wait_send())


def finish_kernel(nsol, nres, dirv, beta_ref, sol_out, res_out, dir_out, ndir, sem):
    copies = [
        pltpu.make_async_copy(nsol, sol_out, sem.at[0]),
        pltpu.make_async_copy(nres, res_out, sem.at[1]),
    ]
    for cp in copies:
        cp.start()
    beta = beta_ref[0:1, 0:1]
    for part in range(2):
        def body(f):
            ndir[part, f] = nres[part, f] + beta * dirv[part, f]

        loop(FEEDS, body)
        cp = pltpu.make_async_copy(ndir.at[part], dir_out.at[part], sem.at[2 + part])
        cp.start()
        copies.append(cp)
    for cp in copies:
        cp.wait()


def per_device(solution_, residual, direction, sample_weight):
    forward, backward = tables()
    window = window_table()
    shape = direction.shape
    vmem = pl.BlockSpec(memory_space=pltpu.VMEM)
    hbm = pl.BlockSpec(memory_space=pl.ANY)
    dma = pltpu.SemaphoreType.DMA
    piece = (2, KHERE, LANES)
    nsol, nres, dirv, beta = pl.pallas_call(
        exchange_kernel,
        name="exchange",
        out_shape=[pltpu.VMEM(shape, F32)] * 3 + [pltpu.VMEM((8, LANES), F32)],
        in_specs=[hbm] * 7,
        out_specs=[vmem] * 4,
        scratch_shapes=[
            pltpu.VMEM((HALF, GROUPS) + piece, F32),
            pltpu.VMEM((HALF, GROUPS) + piece, F32),
            pltpu.VMEM(shape, F32),
            pltpu.VMEM((HALF, RIM, LANES), F32),
            pltpu.VMEM((HALF, RIM, LANES), F32),
            pltpu.VMEM((HALF, RIM, LANES), F32),
            pltpu.VMEM((HALF, RIM, LANES), F32),
            pltpu.VMEM(forward.shape, BF16),
            pltpu.VMEM(backward.shape, BF16),
            pltpu.VMEM(window.shape, F32),
            pltpu.VMEM((ACROSS, BLOCK, SAMPLES), F32),
            pltpu.VMEM((SAMPLES, LANES), F32),
            pltpu.VMEM((RADIX, ROWS, LANES), F32),
            pltpu.VMEM((RADIX, GQ, 2, KHERE, 2 * LANES), BF16),
            pltpu.VMEM((RADIX, ROWS, LANES), F32),
            pltpu.VMEM((RADIX, ROWS, LANES), F32),
            pltpu.VMEM((RADIX, ROWS, 2 * LANES), BF16),
            pltpu.VMEM((RADIX, GQ, 2, KHERE, LANES), F32),
            pltpu.VMEM((2, GROUPS, 1, LANES), F32),
            pltpu.VMEM((2, SEGMENTS, 1, LANES), F32),
            dma((7,)),
            dma((2, HALF)),
            dma((HALF, GROUPS)),
            dma((HALF, GROUPS)),
            dma((HALF, GROUPS)),
            dma((HALF, GROUPS)),
            dma((2, HALF)),
            dma((2, HALF)),
            dma((ACROSS,)),
            dma((ACROSS,)),
            dma((2, GROUPS)),
            dma((2, GROUPS)),
            dma((2, SEGMENTS)),
            dma((2, SEGMENTS)),
        ],
        compiler_params=pltpu.CompilerParams(
            collective_id=0, has_side_effects=True, vmem_limit_bytes=52 * 2**20
        ),
    )(solution_, residual, direction, sample_weight, forward, backward, window)
    inside = [pltpu.with_memory_space_constraint(x, pltpu.VMEM) for x in (nsol, nres, dirv, beta)]
    return pl.pallas_call(
        finish_kernel,
        name="finish",
        out_shape=[jax.ShapeDtypeStruct(shape, F32)] * 3,
        in_specs=[vmem] * 4,
        out_specs=[hbm] * 3,
        scratch_shapes=[pltpu.VMEM(shape, F32), dma((4,))],
        compiler_params=pltpu.CompilerParams(vmem_limit_bytes=24 * 2**20),
    )(*inside)


def solution(mesh):
    placed = P(None, None, "chan", "tm")
    return jax.shard_map(
        per_device,
        mesh=mesh,
        in_specs=(placed, placed, placed, P("tm", "chan", None, None)),
        out_specs=(placed, placed, placed),
        check_vma=False,
    )
```

```python
import math

import jax
import jax.numpy as jnp
import ml_dtypes
import numpy as np
from jax import lax
from jax.experimental import pallas as pl
from jax.experimental.pallas import tpu as pltpu
from jax.sharding import PartitionSpec as P

MESH = pl.DeviceIdType.MESH
F32 = jnp.float32
BF16 = jnp.bfloat16

SAMPLES = 2048
CHANNELS = 1024
TAPS = 4
FEEDS = 8
GROUPS = 32
SEGMENTS = 8
BLOCK = 32
KHERE = 32
HALF = 2
ACROSS = 4
LANES = ACROSS * BLOCK
TILES = SAMPLES // LANES
RIM = 16
MAIN = 2 * LANES
STACK = MAIN + 2 * RIM
RADIX = 8
ROWS = SAMPLES // RADIX
QUARTER = 4
GQ = GROUPS // QUARTER
INNER = GQ * 2 * KHERE
ROOT_HALF = math.sqrt(0.5)
PEERS = GROUPS - 1
ROWS_Z = GROUPS // ACROSS


def tables():
    j = np.arange(CHANNELS // QUARTER)
    r = np.arange(ROWS)
    s = np.arange(RADIX)
    turns = (j[None, None, :] * (RADIX * r[None, :, None] + s[:, None, None])) % SAMPLES
    angle = 2.0 * np.pi * turns / SAMPLES
    scale = 1.0 / math.sqrt(SAMPLES)
    both = np.stack([np.cos(angle) * scale, -np.sin(angle) * scale], axis=1)
    full = both.transpose(0, 1, 3, 2).reshape(RADIX, INNER, ROWS)
    high = full.astype(np.float32).astype(ml_dtypes.bfloat16)
    low = (full - high.astype(np.float64)).astype(np.float32).astype(ml_dtypes.bfloat16)
    forward = np.concatenate([high, low], axis=2)
    backward = np.concatenate([high.transpose(0, 2, 1), low.transpose(0, 2, 1)], axis=2)
    return forward, backward


def window_table():
    position = np.arange(TAPS * SAMPLES, dtype=np.float64)
    taper = 0.5 - 0.5 * np.cos(2.0 * np.pi * position / (TAPS * SAMPLES - 1))
    window = (np.sinc(position / SAMPLES - TAPS / 2) * taper).astype(np.float32)
    window = window.reshape(TAPS, ROWS, RADIX).transpose(0, 2, 1).reshape(TAPS, TILES, 1, LANES)
    return np.ascontiguousarray(np.broadcast_to(window, (TAPS, TILES, 8, LANES)))


def copy_to(src, dst, ssem, rsem, device):
    return pltpu.make_async_remote_copy(
        src_ref=src, dst_ref=dst, send_sem=ssem, recv_sem=rsem, device_id=device, device_id_type=MESH
    )


def loop(n, body, init=None):
    if init is None:
        def plain(i, carry):
            body(i)
            return carry

        lax.fori_loop(0, n, plain, 0)
        return None
    return lax.fori_loop(0, n, body, init)


def fold_rows(x):
    rows, cols = x.shape
    total = None
    for i in range(rows // 8):
        for j in range(cols // LANES):
            y = x[8 * i : 8 * i + 8, LANES * j : LANES * (j + 1)]
            total = y if total is None else total + y
    return total


def exchange_kernel(
    sol_hbm, res_hbm, dir_hbm, wgt_hbm, tf_hbm, tb_hbm, win_hbm,
    nsol, nres, dirv, beta_ref,
    recvf, sendb, recvb, rim_s, rim_r, back_s, back_r, rim_v,
    tf, tb, win, raw, nat, noise, xt, bx, sm, st, bw, vv,
    part_c, part_t,
    load_sem, self_sem, fs, fr, bs, br, rim_sent, rim_got, ns, nr, cs, cr, ts, tr,
):
    c = lax.axis_index("chan")
    t = lax.axis_index("tm")
    z, x_here = c // ACROSS, lax.rem(c, ACROSS)

    some_dev = (lax.rem(c + 1, GROUPS), t)
    t_up = lax.rem(t + 1, SEGMENTS)
    t_down = lax.rem(t + SEGMENTS - 1, SEGMENTS)
    barrier = pltpu.get_barrier_semaphore()

    def greet_chan(i):
        pl.semaphore_signal(
            barrier, inc=1, device_id=(lax.rem(c + i + 1, GROUPS), t), device_id_type=MESH
        )

    def greet_tm(i):
        pl.semaphore_signal(
            barrier, inc=1, device_id=(c, lax.rem(t + i + 1, SEGMENTS)), device_id_type=MESH
        )

    loads = [
        pltpu.make_async_copy(src, dst, load_sem.at[i])
        for i, (src, dst) in enumerate(
            (
                (dir_hbm, dirv),
                (wgt_hbm.at[0, 0], raw.at[x_here]),
                (res_hbm, nres),
                (tf_hbm, tf),
                (win_hbm, win),
                (tb_hbm, tb),
                (sol_hbm, nsol),
            )
        )
    ]
    for cp in loads:
        cp.start()
    loop(GROUPS - 1, greet_chan)
    loop(SEGMENTS - 1, greet_tm)

    def greet_up(i):
        pl.semaphore_signal(barrier, inc=1, device_id=(i, t_up), device_id_type=MESH)

    def greet_down(i):
        pl.semaphore_signal(barrier, inc=1, device_id=(i, t_down), device_id_type=MESH)

    loop(ACROSS, greet_up)

    @pl.when(z == 0)
    def _():
        loop(GROUPS, greet_down)

    def frames_of(zz):
        return pl.ds(pl.multiple_of(zz * LANES, LANES), LANES)

    def forward_copy(h, i):
        d = lax.rem(c + i + 1, GROUPS)
        src = dirv.at[:, HALF * lax.rem(d, ACROSS) + h, :, frames_of(d // ACROSS)]
        return copy_to(src, recvf.at[h, c], fs.at[h], fr.at[h], (d, t))

    def forward_all(h):
        some = recvf.at[h, pl.ds(0, GROUPS - 1)]
        return copy_to(some, some, fs.at[h], fr.at[h], some_dev)

    def backward_copy(h, i):
        d = lax.rem(c + i + 1, GROUPS)
        dst = recvb.at[:, HALF * x_here + h, :, frames_of(z)]
        return copy_to(sendb.at[h, d], dst, bs.at[h], br.at[h], (d, t))

    def backward_all(h):
        some = sendb.at[h, pl.ds(0, GROUPS - 1)]
        return copy_to(some, some, bs.at[h], br.at[h], some_dev)

    def noise_copy(i):
        xx = lax.rem(x_here + i + 1, ACROSS)
        return copy_to(raw.at[x_here], raw.at[x_here], ns.at[0], nr.at[0], (z * ACROSS + xx, t))

    def noise_all():
        some = raw.at[pl.ds(0, ACROSS - 1)]
        return copy_to(some, some, ns.at[0], nr.at[0], some_dev)

    def rim_to(n):
        zz, xx = n // ACROSS, lax.rem(n, ACROSS)
        cc = lax.rem((zz + 1) * ACROSS + xx, GROUPS)
        tt = jnp.where(zz == ROWS_Z - 1, t_up, t)
        src = rim_s.at[zz, xx // 2]
        remote = copy_to(src, rim_r.at[c], rim_sent.at[0], rim_got.at[0], (cc, tt))
        return (zz + 1) * ACROSS + xx == c, remote, pltpu.make_async_copy(src, rim_r.at[c], self_sem.at[2, 0])

    def rim_back(n):
        tt = jnp.where(z == 0, t_down, t)
        remote = copy_to(back_s.at[n], back_r.at[c], rim_sent.at[1], rim_got.at[1], (n, tt))
        own = (n == c) & (z > 0)
        return own, remote, pltpu.make_async_copy(back_s.at[n], back_r.at[c], self_sem.at[2, 1])

    def rim_start(which):
        def body(n):
            own, remote, local = which(n)

            @pl.when(own)
            def _():
                local.start()

            @pl.when(jnp.logical_not(own))
            def _():
                remote.start()

        loop(GROUPS, body)

    def rim_wait(k, sent):
        buf = rim_r if k == 0 else back_r

        def whole(n):
            some = buf.at[pl.ds(0, n)]
            cp = copy_to(some, some, rim_sent.at[k], rim_got.at[k], some_dev)
            if sent:
                cp.wait_send()
            else:
                cp.wait_recv()

        @pl.when(z == 0)
        def _():
            whole(GROUPS)

        @pl.when(z > 0)
        def _():
            whole(PEERS)
            if not sent:
                pltpu.make_async_copy(buf.at[c], buf.at[c], self_sem.at[2, k]).wait()

    here = (HALF * x_here, frames_of(z))
    self_f = [
        pltpu.make_async_copy(dirv.at[:, here[0] + h, :, here[1]], recvf.at[h, c], self_sem.at[0, h])
        for h in range(HALF)
    ]
    self_b = [
        pltpu.make_async_copy(sendb.at[h, c], recvb.at[:, here[0] + h, :, here[1]], self_sem.at[1, h])
        for h in range(HALF)
    ]

    loads[0].wait()
    for h in range(HALF):
        self_f[h].start()
    pl.semaphore_wait(barrier, PEERS + SEGMENTS - 1 + ACROSS + jnp.where(z == 0, GROUPS, 0))
    loop(GROUPS - 1, lambda i: forward_copy(0, i).start())

    def pack_rim(n):
        zz, fh = n // 2, lax.rem(n, 2)
        for part in range(2):
            y = jnp.concatenate([dirv[part, 4 * fh + f, :, frames_of(zz)] for f in range(4)], axis=0).T
            rim_s[zz, fh, TAPS * part : TAPS * (part + 1), :] = y[LANES - TAPS :, :]

    loop(2 * ROWS_Z, pack_rim)
    rim_start(rim_to)
    loads[1].wait()
    loop(ACROSS - 1, lambda i: noise_copy(i).start())
    loop(GROUPS - 1, lambda i: forward_copy(1, i).start())

    loads[2].wait()

    def square(i, acc):
        part, f = i // FEEDS, lax.rem(i, FEEDS)
        y = nres[part, f]
        return acc + fold_rows(y * y)

    norm_part = loop(2 * FEEDS, square, jnp.zeros((8, LANES), F32))

    noise_all().wait_recv()

    def turn(i):
        cols = pl.ds(pl.multiple_of(i * 128, 128), 128)
        nat[cols, :] = jnp.concatenate([raw[q, :, cols] for q in range(ACROSS)], axis=0).T

    loop(SAMPLES // 128, turn)
    for n in range(TILES):
        first = n // 2 + (n % 2) * (SAMPLES // 2)
        noise[n] = nat[pl.ds(first, LANES, stride=RADIX), :].T
    for cp in loads[3:]:
        cp.wait()

    keep_down = jnp.where((z == 0) & (t == 0), 0.0, 1.0).astype(F32)
    blank = jnp.zeros((8, LANES), F32)
    for n in range(TILES):
        st[n, 0:8, :] = blank
        st[n, 8 + LANES : 16 + LANES, :] = blank

    def split(x):
        high = x.astype(BF16)
        return high, (x - high.astype(F32)).astype(BF16)

    def quadrants(x):
        cols = x.shape[1] // 2

        def joined(a, b, n):
            return (x[a : a + n, :cols] + x[a : a + n, cols:]) + (x[b : b + n, :cols] + x[b : b + n, cols:])

        return joined(0, LANES, LANES), joined(MAIN, MAIN + RIM, 8)

    def rim_store(ref, s, cols, x):
        high, low = split(jnp.concatenate([x, jnp.zeros((RIM - 8, LANES), F32)], axis=0))
        ref[s, MAIN : MAIN + RIM, cols] = high
        ref[s, MAIN + RIM : STACK, cols] = low

    lane8 = lax.broadcasted_iota(jnp.int32, (8, LANES), 1)
    odd_x = jnp.full((8, LANES), lax.rem(x_here, 2), jnp.int32) == 1

    def rolled(x, by):
        by = by % LANES
        return pltpu.roll(x, by, 1) if by else x

    RB = 16

    def turned(re, im):
        def pairs(a, b):
            return [
                (re[a] + re[b], im[a] + im[b]),
                (re[a] - im[b], im[a] + re[b]),
                (re[a] - re[b], im[a] - im[b]),
                (re[a] + im[b], im[a] - re[b]),
            ]

        u, v = pairs(0, 2), pairs(1, 3)
        w = [
            v[0],
            ((v[1][0] - v[1][1]) * ROOT_HALF, (v[1][0] + v[1][1]) * ROOT_HALF),
            (-v[2][1], v[2][0]),
            (-(v[3][0] + v[3][1]) * ROOT_HALF, (v[3][0] - v[3][1]) * ROOT_HALF),
        ]
        return u, w

    def fold_in(h):
        def transpose(n):
            p, jb = n // 2, lax.rem(n, 2)
            for part in range(2):
                y = [recvf[h, p * GQ + jb * 4 + g, part] for g in range(4)]
                xt[p, part, jb] = jnp.concatenate(y, axis=0).T

        loop(2 * QUARTER, transpose)

        def body(n):
            jb, i = n // (LANES // RB), lax.rem(n, LANES // RB)
            rows = pl.ds(pl.multiple_of(i * RB, RB), RB)
            low_rows = pl.ds(pl.multiple_of(LANES + i * RB, RB), RB)
            re = [xt[p, 0, jb, rows, :] for p in range(QUARTER)]
            im = [xt[p, 1, jb, rows, :] for p in range(QUARTER)]

            u, w = turned(re, im)
            for s in range(4):
                for part in range(2):
                    cols = pl.ds(pl.multiple_of(part * 2 * LANES + jb * LANES, LANES), LANES)
                    for ss, y in ((s, u[s][part] + w[s][part]), (s + 4, u[s][part] - w[s][part])):
                        bx[ss, rows, cols], bx[ss, low_rows, cols] = split(y)

        loop(2 * LANES // RB, body)
        for jb in range(2):
            re, im = [], []
            for p in range(QUARTER):
                total = blank
                for g in range(4):
                    y = rim_r[p * GQ + jb * 4 + g]
                    y = jnp.where(odd_x, pltpu.roll(y, LANES // 2, 1), y)
                    total = jnp.where(lane8 // KHERE == g, rolled(y, KHERE * (g - h)), total)
                re.append(total)
                im.append(jnp.concatenate([total[TAPS:], total[:TAPS]], axis=0))
            u, w = turned(re, im)
            for s in range(4):
                for part in range(2):
                    cols = slice((2 * part + jb) * LANES, (2 * part + jb + 1) * LANES)
                    rim_store(bx, s, cols, u[s][part] + w[s][part])
                    rim_store(bx, s + 4, cols, u[s][part] - w[s][part])

    def to_samples():
        def body(s):
            y, rim = quadrants(jnp.dot(bx[s], tf[s], preferred_element_type=F32))
            for half in range(2):
                cols = slice(half * LANES, (half + 1) * LANES)
                sm[2 * s + half, 8 : 8 + LANES, :] = y[:, cols]
                sm[2 * s + half, 8 - TAPS : 8, :] = rim[:TAPS, cols] * keep_down

        loop(RADIX, body)

    def make_stream(acc):
        def body(n, acc):
            w = [win[k, n] for k in range(TAPS)]
            for i in range(LANES // 8):
                total = w[0] * sm[n, 8 + 8 * i : 16 + 8 * i, :]
                for k in range(1, TAPS):
                    total = total + w[k] * sm[n, 8 + 8 * i - k : 16 + 8 * i - k, :]
                y = noise[n, 8 * i : 8 * i + 8, :] * total
                st[n, 8 * i + 8 : 8 * i + 16, :] = y
                acc = acc + y * total
            return acc

        return loop(TILES, body, acc)

    def make_weighted():
        def body(s):
            for half in range(2):
                n = 2 * s + half
                cols = slice(half * LANES, (half + 1) * LANES)
                w = [jnp.concatenate([win[k, n]] * (RB // 8), axis=0) for k in range(TAPS)]
                for i in range(LANES // RB):
                    total = w[0] * st[n, 8 + RB * i : 8 + RB * (i + 1), :]
                    for k in range(1, TAPS):
                        total = total + w[k] * st[n, 8 + RB * i + k : 8 + RB * (i + 1) + k, :]
                    high, low = split(total)
                    bw[s, RB * i : RB * (i + 1), cols] = high
                    bw[s, LANES + RB * i : LANES + RB * (i + 1), cols] = low
                rim = win[0, n] * st[n, 0:8, :]
                for k in range(1, TAPS):
                    rim = rim + win[k, n] * st[n, k : 8 + k, :]
                rim_store(bw, s, cols, rim)

        loop(RADIX, body)

    def to_spectra():
        def body(s):
            y, rim = quadrants(jnp.dot(bw[s], tb[s], preferred_element_type=F32))
            vv[s, :LANES, :] = y
            vv[s, LANES:, :] = rim

        loop(RADIX, body)

    def joined_image(re, im):
        ar = [re[s] + re[s + 4] for s in range(4)]
        ai = [im[s] + im[s + 4] for s in range(4)]
        dr = [re[s] - re[s + 4] for s in range(4)]
        di = [im[s] - im[s + 4] for s in range(4)]
        one = ((dr[1] + di[1]) * ROOT_HALF, (di[1] - dr[1]) * ROOT_HALF)
        one3 = ((di[1] - dr[1]) * ROOT_HALF, -(di[1] + dr[1]) * ROOT_HALF)
        three = ((di[3] - dr[3]) * ROOT_HALF, -(di[3] + dr[3]) * ROOT_HALF)
        three3 = ((dr[3] + di[3]) * ROOT_HALF, (di[3] - dr[3]) * ROOT_HALF)
        return [
            ((ar[0] + ar[2]) + (ar[1] + ar[3]), (ai[0] + ai[2]) + (ai[1] + ai[3])),
            ((dr[0] + di[2]) + (one[0] + three[0]), (di[0] - dr[2]) + (one[1] + three[1])),
            ((ar[0] - ar[2]) + (ai[1] - ai[3]), (ai[0] - ai[2]) + (ar[3] - ar[1])),
            ((dr[0] - di[2]) + (one3[0] + three3[0]), (di[0] + dr[2]) + (one3[1] + three3[1])),
        ]

    def fold_out(h):
        def body(n):
            jb, i = n // (LANES // RB), lax.rem(n, LANES // RB)
            rows = pl.ds(pl.multiple_of(i * RB, RB), RB)
            cols = [pl.ds(pl.multiple_of((2 * part + jb) * LANES, LANES), LANES) for part in range(2)]
            re = [vv[s, rows, cols[0]] for s in range(RADIX)]
            im = [vv[s, rows, cols[1]] for s in range(RADIX)]
            image = joined_image(re, im)
            for p in range(QUARTER):
                for part in range(2):
                    xt[p, part, jb, rows, :] = image[p][part]

        loop(2 * LANES // RB, body)

        for jb in range(2):
            cols = [slice((2 * part + jb) * LANES, (2 * part + jb + 1) * LANES) for part in range(2)]
            image = joined_image(*[[vv[s, LANES:, cols[part]] for s in range(RADIX)] for part in range(2)])
            for p in range(QUARTER):
                rim_v[h, p, jb] = jnp.concatenate([image[p][0][TAPS:], image[p][1][TAPS:]], axis=0)

        def transpose(n):
            p, jb = n // 2, lax.rem(n, 2)
            for part in range(2):
                y = xt[p, part, jb].T
                for g in range(4):
                    sendb[h, p * GQ + jb * 4 + g, part] = y[KHERE * g : KHERE * (g + 1), :]

        loop(2 * QUARTER, transpose)

    def tm_copy(rnd, i):
        d = lax.rem(t + i + 1, SEGMENTS)
        return copy_to(part_t.at[rnd, t], part_t.at[rnd, t], ts.at[rnd], tr.at[rnd], (c, d))

    def tm_all(rnd):
        some = part_t.at[rnd, pl.ds(0, SEGMENTS - 1)]
        return copy_to(some, some, ts.at[rnd], tr.at[rnd], some_dev)

    def chan_copy(rnd, i):
        d = lax.rem(c + i + 1, GROUPS)
        return copy_to(part_c.at[rnd, c], part_c.at[rnd, c], cs.at[rnd], cr.at[rnd], (d, t))

    def chan_all(rnd):
        some = part_c.at[rnd, pl.ds(0, GROUPS - 1)]
        return copy_to(some, some, cs.at[rnd], cr.at[rnd], some_dev)

    def sum_start(rnd, row):
        part_t[rnd, t] = row
        loop(SEGMENTS - 1, lambda i: tm_copy(rnd, i).start())

    def sum_middle(rnd):
        tm_all(rnd).wait_recv()
        part_c[rnd, c] = jnp.sum(part_t[rnd], axis=0)
        loop(GROUPS - 1, lambda i: chan_copy(rnd, i).start())

    def sum_end(rnd):
        chan_all(rnd).wait_recv()
        return jnp.sum(part_c[rnd], axis=0)

    def sum_sent(rnd):
        tm_all(rnd).wait_send()
        chan_all(rnd).wait_send()

    lane_row = lax.broadcasted_iota(jnp.int32, (1, LANES), 1)

    def both(first, second):
        a = jnp.sum(first, axis=0, keepdims=True)
        b = jnp.sum(second, axis=0, keepdims=True)
        half = LANES // 2
        return jnp.where(lane_row < half, a + pltpu.roll(a, half, 1), b + pltpu.roll(b, half, 1))

    curve = jnp.zeros((8, LANES), F32)
    for h in range(HALF):
        self_f[h].wait()
        forward_all(h).wait_recv()
        if h == 0:
            rim_wait(0, False)
        fold_in(h)
        to_samples()
        curve = make_stream(curve)
        if h == HALF - 1:
            sum_start(0, both(norm_part, curve))
        make_weighted()
        to_spectra()
        fold_out(h)
        if h == HALF - 1:
            sum_middle(0)
            for n in range(GROUPS):
                p, jb, g = n // 8, (n // 4) % 2, n % 4
                first, second = rolled(rim_v[0, p, jb], -KHERE * g), rolled(rim_v[1, p, jb], KHERE - KHERE * g)
                back_s[n] = jnp.where(lane8 < KHERE, first, second)
            rim_start(rim_back)
        loop(GROUPS - 1, lambda i: backward_copy(h, i).start())
        self_b[h].start()

    sums = sum_end(0)
    zero = jnp.zeros((1, LANES), F32)
    norm_now = jnp.sum(jnp.where(lane_row < LANES // 2, sums, zero), axis=1, keepdims=True)
    alpha = norm_now / jnp.sum(jnp.where(lane_row < LANES // 2, zero, sums), axis=1, keepdims=True)

    def step_solution(i):
        part, f = i // FEEDS, lax.rem(i, FEEDS)
        nsol[part, f] = nsol[part, f] + alpha * dirv[part, f]

    loop(2 * FEEDS, step_solution)

    rim_wait(1, False)

    def take_rim(zz):
        above = lax.rem(zz + 1, ROWS_Z) * ACROSS
        keep = jnp.where((zz == ROWS_Z - 1) & (t == SEGMENTS - 1), 0.0, 1.0).astype(F32)
        for h in range(HALF):
            total = blank
            for xx in range(ACROSS):
                total = jnp.where(lane8 // KHERE == xx, rolled(back_r[above + xx], KHERE * (xx - h)), total)
            total = total * (keep * alpha)
            for part in range(2):
                last = total[TAPS * part : TAPS * (part + 1)]
                y = jnp.concatenate([jnp.zeros((LANES - TAPS, LANES), F32), last], axis=0).T
                for xx in range(ACROSS):
                    f = HALF * xx + h
                    nres[part, f, :, frames_of(zz)] = (
                        nres[part, f, :, frames_of(zz)] - y[KHERE * xx : KHERE * (xx + 1), :]
                    )

    loop(ROWS_Z, take_rim)

    norm_next = jnp.zeros((8, LANES), F32)
    for h in range(HALF):
        self_b[h].wait()
        backward_all(h).wait_recv()

        def update(i, acc):
            part, f = i // ACROSS, HALF * lax.rem(i, ACROSS) + h
            y = nres[part, f] - alpha * recvb[part, f]
            nres[part, f] = y
            return acc + fold_rows(y * y)

        norm_next = loop(2 * ACROSS, update, norm_next)

    sum_start(1, jnp.sum(norm_next, axis=0, keepdims=True))
    sum_middle(1)
    total = jnp.sum(sum_end(1), axis=1, keepdims=True)
    beta_ref[...] = jnp.broadcast_to(total / norm_now, (8, LANES))
    for h in range(HALF):
        forward_all(h).wait_send()
        backward_all(h).wait_send()
    noise_all().wait_send()
    rim_wait(0, True)
    rim_wait(1, True)
    sum_sent(0)
    sum_sent(1)


def finish_kernel(nsol, nres, dirv, beta_ref, sol_out, res_out, dir_out, ndir, sem):
    copies = [
        pltpu.make_async_copy(nsol, sol_out, sem.at[0]),
        pltpu.make_async_copy(nres, res_out, sem.at[1]),
    ]
    for cp in copies:
        cp.start()
    beta = beta_ref[0:1, 0:1]
    for part in range(2):
        def body(f):
            ndir[part, f] = nres[part, f] + beta * dirv[part, f]

        loop(FEEDS, body)
        cp = pltpu.make_async_copy(ndir.at[part], dir_out.at[part], sem.at[2 + part])
        cp.start()
        copies.append(cp)
    for cp in copies:
        cp.wait()


def per_device(solution_, residual, direction, sample_weight):
    forward, backward = tables()
    window = window_table()
    shape = direction.shape
    vmem = pl.BlockSpec(memory_space=pltpu.VMEM)
    hbm = pl.BlockSpec(memory_space=pl.ANY)
    dma = pltpu.SemaphoreType.DMA
    piece = (2, KHERE, LANES)
    nsol, nres, dirv, beta = pl.pallas_call(
        exchange_kernel,
        name="exchange",
        out_shape=[pltpu.VMEM(shape, F32)] * 3 + [pltpu.VMEM((8, LANES), F32)],
        in_specs=[hbm] * 7,
        out_specs=[vmem] * 4,
        scratch_shapes=[
            pltpu.VMEM((HALF, GROUPS) + piece, F32),
            pltpu.VMEM((HALF, GROUPS) + piece, F32),
            pltpu.VMEM(shape, F32),
            pltpu.VMEM((ROWS_Z, 2, 8, LANES), F32),
            pltpu.VMEM((GROUPS, 8, LANES), F32),
            pltpu.VMEM((GROUPS, 8, LANES), F32),
            pltpu.VMEM((GROUPS, 8, LANES), F32),
            pltpu.VMEM((HALF, QUARTER, 2, 8, LANES), F32),
            pltpu.VMEM(forward.shape, BF16),
            pltpu.VMEM(backward.shape, BF16),
            pltpu.VMEM(window.shape, F32),
            pltpu.VMEM((ACROSS, BLOCK, SAMPLES), F32),
            pltpu.VMEM((SAMPLES, LANES), F32),
            pltpu.VMEM((TILES, LANES, LANES), F32),
            pltpu.VMEM((QUARTER, 2, 2, LANES, LANES), F32),
            pltpu.VMEM((RADIX, STACK, INNER), BF16),
            pltpu.VMEM((TILES, LANES + 8, LANES), F32),
            pltpu.VMEM((TILES, LANES + 16, LANES), F32),
            pltpu.VMEM((RADIX, STACK, ROWS), BF16),
            pltpu.VMEM((RADIX, LANES + 8, INNER), F32),
            pltpu.VMEM((2, GROUPS, 1, LANES), F32),
            pltpu.VMEM((2, SEGMENTS, 1, LANES), F32),
            dma((7,)),
            dma((3, HALF)),
            dma((HALF,)),
            dma((HALF,)),
            dma((HALF,)),
            dma((HALF,)),
            dma((2,)),
            dma((2,)),
            dma((1,)),
            dma((1,)),
            dma((2,)),
            dma((2,)),
            dma((2,)),
            dma((2,)),
        ],
        compiler_params=pltpu.CompilerParams(
            collective_id=0, has_side_effects=True, vmem_limit_bytes=52 * 2**20
        ),
    )(solution_, residual, direction, sample_weight, forward, backward, window)
    inside = [pltpu.with_memory_space_constraint(x, pltpu.VMEM) for x in (nsol, nres, dirv, beta)]
    return pl.pallas_call(
        finish_kernel,
        name="finish",
        out_shape=[jax.ShapeDtypeStruct(shape, F32)] * 3,
        in_specs=[vmem] * 4,
        out_specs=[hbm] * 3,
        scratch_shapes=[pltpu.VMEM(shape, F32), dma((4,))],
        compiler_params=pltpu.CompilerParams(vmem_limit_bytes=24 * 2**20),
    )(*inside)


def solution(mesh):
    placed = P(None, None, "chan", "tm")
    return jax.shard_map(
        per_device,
        mesh=mesh,
        in_specs=(placed, placed, placed, P("tm", "chan", None, None)),
        out_specs=(placed, placed, placed),
        check_vma=False,
    )
```

```python
import math

import jax
import jax.numpy as jnp
import ml_dtypes
import numpy as np
from jax import lax
from jax.experimental import pallas as pl
from jax.experimental.pallas import tpu as pltpu
from jax.sharding import PartitionSpec as P

MESH = pl.DeviceIdType.MESH
F32 = jnp.float32
BF16 = jnp.bfloat16

SAMPLES = 2048
CHANNELS = 1024
TAPS = 4
FEEDS = 8
GROUPS = 32
SEGMENTS = 8
BLOCK = 32
KHERE = 32
HALF = 2
ACROSS = 4
LANES = ACROSS * BLOCK
TILES = SAMPLES // LANES
RIM = 16
MAIN = 2 * LANES
STACK = MAIN + 2 * RIM
RADIX = 8
ROWS = SAMPLES // RADIX
QUARTER = 4
GQ = GROUPS // QUARTER
INNER = GQ * 2 * KHERE
ROOT_HALF = math.sqrt(0.5)
PEERS = GROUPS - 1
ROWS_Z = GROUPS // ACROSS


def tables():
    j = np.arange(CHANNELS // QUARTER)
    r = np.arange(ROWS)
    s = np.arange(RADIX)
    turns = (j[None, None, :] * (RADIX * r[None, :, None] + s[:, None, None])) % SAMPLES
    angle = 2.0 * np.pi * turns / SAMPLES
    scale = 1.0 / math.sqrt(SAMPLES)
    both = np.stack([np.cos(angle) * scale, -np.sin(angle) * scale], axis=1)
    full = both.transpose(0, 1, 3, 2).reshape(RADIX, INNER, ROWS)
    high = full.astype(np.float32).astype(ml_dtypes.bfloat16)
    low = (full - high.astype(np.float64)).astype(np.float32).astype(ml_dtypes.bfloat16)
    forward = np.concatenate([high, low], axis=2)
    backward = np.concatenate([high.transpose(0, 2, 1), low.transpose(0, 2, 1)], axis=2)
    return forward, backward


def window_table():
    position = np.arange(TAPS * SAMPLES, dtype=np.float64)
    taper = 0.5 - 0.5 * np.cos(2.0 * np.pi * position / (TAPS * SAMPLES - 1))
    window = (np.sinc(position / SAMPLES - TAPS / 2) * taper).astype(np.float32)
    window = window.reshape(TAPS, ROWS, RADIX).transpose(0, 2, 1).reshape(TAPS, TILES, 1, LANES)
    return np.ascontiguousarray(np.broadcast_to(window, (TAPS, TILES, 8, LANES)))


def copy_to(src, dst, ssem, rsem, device):
    return pltpu.make_async_remote_copy(
        src_ref=src, dst_ref=dst, send_sem=ssem, recv_sem=rsem, device_id=device, device_id_type=MESH
    )


def loop(n, body, init=None):
    if init is None:
        def plain(i, carry):
            body(i)
            return carry

        lax.fori_loop(0, n, plain, 0)
        return None
    return lax.fori_loop(0, n, body, init)


def fold_rows(x):
    rows, cols = x.shape
    total = None
    for i in range(rows // 8):
        for j in range(cols // LANES):
            y = x[8 * i : 8 * i + 8, LANES * j : LANES * (j + 1)]
            total = y if total is None else total + y
    return total


def exchange_kernel(
    sol_hbm, res_hbm, dir_hbm, wgt_hbm, tf_hbm, tb_hbm, win_hbm,
    nsol, nres, dirv, beta_ref,
    recvf, sendb, recvb, rim_s, rim_r, back_s, back_r, rim_v,
    tf, tb, win, raw, nat, noise, xt, bx, sm, st, bw, vv,
    part_c, part_t,
    load_sem, self_sem, fs, fr, bs, br, rim_sent, rim_got, ns, nr, cs, cr, ts, tr,
):
    c = lax.axis_index("chan")
    t = lax.axis_index("tm")
    z, x_here = c // ACROSS, lax.rem(c, ACROSS)

    some_dev = (lax.rem(c + 1, GROUPS), t)
    t_up = lax.rem(t + 1, SEGMENTS)
    t_down = lax.rem(t + SEGMENTS - 1, SEGMENTS)
    barrier = pltpu.get_barrier_semaphore()

    def greet_chan(i):
        pl.semaphore_signal(
            barrier, inc=1, device_id=(lax.rem(c + i + 1, GROUPS), t), device_id_type=MESH
        )

    def greet_tm(i):
        pl.semaphore_signal(
            barrier, inc=1, device_id=(c, lax.rem(t + i + 1, SEGMENTS)), device_id_type=MESH
        )

    loads = [
        pltpu.make_async_copy(src, dst, load_sem.at[i])
        for i, (src, dst) in enumerate(
            (
                (dir_hbm, dirv),
                (wgt_hbm.at[0, 0], raw.at[x_here]),
                (res_hbm, nres),
                (tf_hbm, tf),
                (win_hbm, win),
                (tb_hbm, tb),
                (sol_hbm, nsol),
            )
        )
    ]
    for cp in loads:
        cp.start()
    loop(GROUPS - 1, greet_chan)
    loop(SEGMENTS - 1, greet_tm)

    def greet_up(i):
        pl.semaphore_signal(barrier, inc=1, device_id=(i, t_up), device_id_type=MESH)

    def greet_down(i):
        pl.semaphore_signal(barrier, inc=1, device_id=(i, t_down), device_id_type=MESH)

    loop(ACROSS, greet_up)

    @pl.when(z == 0)
    def _():
        loop(GROUPS, greet_down)

    def frames_of(zz):
        return pl.ds(pl.multiple_of(zz * LANES, LANES), LANES)

    def forward_copy(h, i):
        d = lax.rem(c + i + 1, GROUPS)
        src = dirv.at[:, HALF * lax.rem(d, ACROSS) + h, :, frames_of(d // ACROSS)]
        return copy_to(src, recvf.at[h, c], fs.at[h], fr.at[h], (d, t))

    def forward_all(h):
        some = recvf.at[h, pl.ds(0, GROUPS - 1)]
        return copy_to(some, some, fs.at[h], fr.at[h], some_dev)

    def backward_copy(h, i):
        d = lax.rem(c + i + 1, GROUPS)
        dst = recvb.at[:, HALF * x_here + h, :, frames_of(z)]
        return copy_to(sendb.at[h, d], dst, bs.at[h], br.at[h], (d, t))

    def backward_all(h):
        some = sendb.at[h, pl.ds(0, GROUPS - 1)]
        return copy_to(some, some, bs.at[h], br.at[h], some_dev)

    def noise_copy(i):
        xx = lax.rem(x_here + i + 1, ACROSS)
        return copy_to(raw.at[x_here], raw.at[x_here], ns.at[0], nr.at[0], (z * ACROSS + xx, t))

    def noise_all():
        some = raw.at[pl.ds(0, ACROSS - 1)]
        return copy_to(some, some, ns.at[0], nr.at[0], some_dev)

    def rim_to(n):
        zz, xx = n // ACROSS, lax.rem(n, ACROSS)
        cc = lax.rem((zz + 1) * ACROSS + xx, GROUPS)
        tt = jnp.where(zz == ROWS_Z - 1, t_up, t)
        src = rim_s.at[zz, xx]
        remote = copy_to(src, rim_r.at[c], rim_sent.at[0], rim_got.at[0], (cc, tt))
        return (zz + 1) * ACROSS + xx == c, remote, pltpu.make_async_copy(src, rim_r.at[c], self_sem.at[2, 0])

    def rim_back(n):
        tt = jnp.where(z == 0, t_down, t)
        remote = copy_to(back_s.at[n], back_r.at[c], rim_sent.at[1], rim_got.at[1], (n, tt))
        own = (n == c) & (z > 0)
        return own, remote, pltpu.make_async_copy(back_s.at[n], back_r.at[c], self_sem.at[2, 1])

    def rim_start(which):
        def body(n):
            own, remote, local = which(n)

            @pl.when(own)
            def _():
                local.start()

            @pl.when(jnp.logical_not(own))
            def _():
                remote.start()

        loop(GROUPS, body)

    def rim_wait(k, sent):
        buf = rim_r if k == 0 else back_r

        def whole(n):
            some = buf.at[pl.ds(0, n)]
            cp = copy_to(some, some, rim_sent.at[k], rim_got.at[k], some_dev)
            if sent:
                cp.wait_send()
            else:
                cp.wait_recv()

        @pl.when(z == 0)
        def _():
            whole(GROUPS)

        @pl.when(z > 0)
        def _():
            whole(PEERS)
            if not sent:
                pltpu.make_async_copy(buf.at[c], buf.at[c], self_sem.at[2, k]).wait()

    here = (HALF * x_here, frames_of(z))
    self_f = [
        pltpu.make_async_copy(dirv.at[:, here[0] + h, :, here[1]], recvf.at[h, c], self_sem.at[0, h])
        for h in range(HALF)
    ]
    self_b = [
        pltpu.make_async_copy(sendb.at[h, c], recvb.at[:, here[0] + h, :, here[1]], self_sem.at[1, h])
        for h in range(HALF)
    ]

    loads[0].wait()
    for h in range(HALF):
        self_f[h].start()
    pl.semaphore_wait(barrier, PEERS + SEGMENTS - 1 + ACROSS + jnp.where(z == 0, GROUPS, 0))
    loop(GROUPS - 1, lambda i: forward_copy(0, i).start())

    low8 = lax.broadcasted_iota(jnp.int32, (8, LANES), 1) < LANES // 2

    def pack_rim(n):
        zz, fh = n // 2, lax.rem(n, 2)
        y = [
            jnp.concatenate([dirv[part, 4 * fh + f, :, frames_of(zz)] for f in range(4)], axis=0).T[LANES - 8 :]
            for part in range(2)
        ]
        rim_s[zz, 2 * fh] = jnp.where(low8, y[0], pltpu.roll(y[1], LANES // 2, 1))[TAPS:]
        rim_s[zz, 2 * fh + 1] = jnp.where(low8, pltpu.roll(y[0], LANES // 2, 1), y[1])[TAPS:]

    loop(2 * ROWS_Z, pack_rim)
    rim_start(rim_to)
    loads[1].wait()
    loop(ACROSS - 1, lambda i: noise_copy(i).start())
    loop(GROUPS - 1, lambda i: forward_copy(1, i).start())

    loads[2].wait()

    def square(i, acc):
        part, f = i // FEEDS, lax.rem(i, FEEDS)
        y = nres[part, f]
        return acc + fold_rows(y * y)

    norm_part = loop(2 * FEEDS, square, jnp.zeros((8, LANES), F32))

    noise_all().wait_recv()

    def turn(i):
        cols = pl.ds(pl.multiple_of(i * 128, 128), 128)
        nat[cols, :] = jnp.concatenate([raw[q, :, cols] for q in range(ACROSS)], axis=0).T

    loop(SAMPLES // 128, turn)
    for n in range(TILES):
        first = n // 2 + (n % 2) * (SAMPLES // 2)
        noise[n] = nat[pl.ds(first, LANES, stride=RADIX), :].T
    for cp in loads[3:]:
        cp.wait()

    keep_down = jnp.where((z == 0) & (t == 0), 0.0, 1.0).astype(F32)
    blank = jnp.zeros((8, LANES), F32)
    for n in range(TILES):
        st[n, 0:8, :] = blank
        st[n, 8 + LANES : 16 + LANES, :] = blank

    def split(x):
        high = x.astype(BF16)
        return high, (x - high.astype(F32)).astype(BF16)

    def quadrants(x):
        cols = x.shape[1] // 2

        def joined(a, b, n):
            return (x[a : a + n, :cols] + x[a : a + n, cols:]) + (x[b : b + n, :cols] + x[b : b + n, cols:])

        return joined(0, LANES, LANES), joined(MAIN, MAIN + RIM, 8)

    def rim_store(ref, s, cols, x):
        high, low = split(jnp.concatenate([x, jnp.zeros((RIM - 8, LANES), F32)], axis=0))
        ref[s, MAIN : MAIN + RIM, cols] = high
        ref[s, MAIN + RIM : STACK, cols] = low

    lane8 = lax.broadcasted_iota(jnp.int32, (8, LANES), 1)

    def rolled(x, by):
        by = by % LANES
        return pltpu.roll(x, by, 1) if by else x

    RB = 16

    def turned(re, im):
        def pairs(a, b):
            return [
                (re[a] + re[b], im[a] + im[b]),
                (re[a] - im[b], im[a] + re[b]),
                (re[a] - re[b], im[a] - im[b]),
                (re[a] + im[b], im[a] - re[b]),
            ]

        u, v = pairs(0, 2), pairs(1, 3)
        w = [
            v[0],
            ((v[1][0] - v[1][1]) * ROOT_HALF, (v[1][0] + v[1][1]) * ROOT_HALF),
            (-v[2][1], v[2][0]),
            (-(v[3][0] + v[3][1]) * ROOT_HALF, (v[3][0] - v[3][1]) * ROOT_HALF),
        ]
        return u, w

    def fold_in(h):
        def transpose(n):
            p, jb = n // 2, lax.rem(n, 2)
            for part in range(2):
                y = [recvf[h, p * GQ + jb * 4 + g, part] for g in range(4)]
                xt[p, part, jb] = jnp.concatenate(y, axis=0).T

        loop(2 * QUARTER, transpose)

        def body(n):
            jb, i = n // (LANES // RB), lax.rem(n, LANES // RB)
            rows = pl.ds(pl.multiple_of(i * RB, RB), RB)
            low_rows = pl.ds(pl.multiple_of(LANES + i * RB, RB), RB)
            re = [xt[p, 0, jb, rows, :] for p in range(QUARTER)]
            im = [xt[p, 1, jb, rows, :] for p in range(QUARTER)]

            u, w = turned(re, im)
            for s in range(4):
                for part in range(2):
                    cols = pl.ds(pl.multiple_of(part * 2 * LANES + jb * LANES, LANES), LANES)
                    for ss, y in ((s, u[s][part] + w[s][part]), (s + 4, u[s][part] - w[s][part])):
                        bx[ss, rows, cols], bx[ss, low_rows, cols] = split(y)

        loop(2 * LANES // RB, body)
        for jb in range(2):
            re, im = [], []
            for p in range(QUARTER):
                both_parts = [blank, blank]
                for g in range(4):
                    y = rim_r[p * GQ + jb * 4 + g]
                    y = jnp.concatenate([y, y], axis=0)
                    for part in range(2):
                        moved = rolled(y, KHERE * (g - h - 2 * part))
                        both_parts[part] = jnp.where(lane8 // KHERE == g, moved, both_parts[part])
                re.append(both_parts[0])
                im.append(both_parts[1])
            u, w = turned(re, im)
            for s in range(4):
                for part in range(2):
                    cols = slice((2 * part + jb) * LANES, (2 * part + jb + 1) * LANES)
                    rim_store(bx, s, cols, u[s][part] + w[s][part])
                    rim_store(bx, s + 4, cols, u[s][part] - w[s][part])

    def to_samples():
        def body(s):
            y, rim = quadrants(jnp.dot(bx[s], tf[s], preferred_element_type=F32))
            for half in range(2):
                cols = slice(half * LANES, (half + 1) * LANES)
                sm[2 * s + half, 8 : 8 + LANES, :] = y[:, cols]
                sm[2 * s + half, 8 - TAPS : 8, :] = rim[:TAPS, cols] * keep_down

        loop(RADIX, body)

    def make_stream(acc):
        def body(n, acc):
            w = [win[k, n] for k in range(TAPS)]
            for i in range(LANES // 8):
                total = w[0] * sm[n, 8 + 8 * i : 16 + 8 * i, :]
                for k in range(1, TAPS):
                    total = total + w[k] * sm[n, 8 + 8 * i - k : 16 + 8 * i - k, :]
                y = noise[n, 8 * i : 8 * i + 8, :] * total
                st[n, 8 * i + 8 : 8 * i + 16, :] = y
                acc = acc + y * total
            return acc

        return loop(TILES, body, acc)

    def make_weighted():
        def body(s):
            for half in range(2):
                n = 2 * s + half
                cols = slice(half * LANES, (half + 1) * LANES)
                w = [jnp.concatenate([win[k, n]] * (RB // 8), axis=0) for k in range(TAPS)]
                for i in range(LANES // RB):
                    total = w[0] * st[n, 8 + RB * i : 8 + RB * (i + 1), :]
                    for k in range(1, TAPS):
                        total = total + w[k] * st[n, 8 + RB * i + k : 8 + RB * (i + 1) + k, :]
                    high, low = split(total)
                    bw[s, RB * i : RB * (i + 1), cols] = high
                    bw[s, LANES + RB * i : LANES + RB * (i + 1), cols] = low
                rim = win[0, n] * st[n, 0:8, :]
                for k in range(1, TAPS):
                    rim = rim + win[k, n] * st[n, k : 8 + k, :]
                rim_store(bw, s, cols, rim)

        loop(RADIX, body)

    def to_spectra():
        def body(s):
            y, rim = quadrants(jnp.dot(bw[s], tb[s], preferred_element_type=F32))
            vv[s, :LANES, :] = y
            vv[s, LANES:, :] = rim

        loop(RADIX, body)

    def joined_image(re, im):
        ar = [re[s] + re[s + 4] for s in range(4)]
        ai = [im[s] + im[s + 4] for s in range(4)]
        dr = [re[s] - re[s + 4] for s in range(4)]
        di = [im[s] - im[s + 4] for s in range(4)]
        one = ((dr[1] + di[1]) * ROOT_HALF, (di[1] - dr[1]) * ROOT_HALF)
        one3 = ((di[1] - dr[1]) * ROOT_HALF, -(di[1] + dr[1]) * ROOT_HALF)
        three = ((di[3] - dr[3]) * ROOT_HALF, -(di[3] + dr[3]) * ROOT_HALF)
        three3 = ((dr[3] + di[3]) * ROOT_HALF, (di[3] - dr[3]) * ROOT_HALF)
        return [
            ((ar[0] + ar[2]) + (ar[1] + ar[3]), (ai[0] + ai[2]) + (ai[1] + ai[3])),
            ((dr[0] + di[2]) + (one[0] + three[0]), (di[0] - dr[2]) + (one[1] + three[1])),
            ((ar[0] - ar[2]) + (ai[1] - ai[3]), (ai[0] - ai[2]) + (ar[3] - ar[1])),
            ((dr[0] - di[2]) + (one3[0] + three3[0]), (di[0] + dr[2]) + (one3[1] + three3[1])),
        ]

    def fold_out(h):
        def body(n):
            jb, i = n // (LANES // RB), lax.rem(n, LANES // RB)
            rows = pl.ds(pl.multiple_of(i * RB, RB), RB)
            cols = [pl.ds(pl.multiple_of((2 * part + jb) * LANES, LANES), LANES) for part in range(2)]
            re = [vv[s, rows, cols[0]] for s in range(RADIX)]
            im = [vv[s, rows, cols[1]] for s in range(RADIX)]
            image = joined_image(re, im)
            for p in range(QUARTER):
                for part in range(2):
                    xt[p, part, jb, rows, :] = image[p][part]

        loop(2 * LANES // RB, body)

        for jb in range(2):
            cols = [slice((2 * part + jb) * LANES, (2 * part + jb + 1) * LANES) for part in range(2)]
            image = joined_image(*[[vv[s, LANES:, cols[part]] for s in range(RADIX)] for part in range(2)])
            for p in range(QUARTER):
                rim_v[h, p, jb] = jnp.concatenate([image[p][0][TAPS:], image[p][1][TAPS:]], axis=0)

        def transpose(n):
            p, jb = n // 2, lax.rem(n, 2)
            for part in range(2):
                y = xt[p, part, jb].T
                for g in range(4):
                    sendb[h, p * GQ + jb * 4 + g, part] = y[KHERE * g : KHERE * (g + 1), :]

        loop(2 * QUARTER, transpose)

    def tm_copy(rnd, i):
        d = lax.rem(t + i + 1, SEGMENTS)
        return copy_to(part_t.at[rnd, t], part_t.at[rnd, t], ts.at[rnd], tr.at[rnd], (c, d))

    def tm_all(rnd):
        some = part_t.at[rnd, pl.ds(0, SEGMENTS - 1)]
        return copy_to(some, some, ts.at[rnd], tr.at[rnd], some_dev)

    def chan_copy(rnd, i):
        d = lax.rem(c + i + 1, GROUPS)
        return copy_to(part_c.at[rnd, c], part_c.at[rnd, c], cs.at[rnd], cr.at[rnd], (d, t))

    def chan_all(rnd):
        some = part_c.at[rnd, pl.ds(0, GROUPS - 1)]
        return copy_to(some, some, cs.at[rnd], cr.at[rnd], some_dev)

    def sum_start(rnd, row):
        part_t[rnd, t] = row
        loop(SEGMENTS - 1, lambda i: tm_copy(rnd, i).start())

    def sum_middle(rnd):
        tm_all(rnd).wait_recv()
        part_c[rnd, c] = jnp.sum(part_t[rnd], axis=0)
        loop(GROUPS - 1, lambda i: chan_copy(rnd, i).start())

    def sum_end(rnd):
        chan_all(rnd).wait_recv()
        return jnp.sum(part_c[rnd], axis=0)

    def sum_sent(rnd):
        tm_all(rnd).wait_send()
        chan_all(rnd).wait_send()

    lane_row = lax.broadcasted_iota(jnp.int32, (1, LANES), 1)

    def both(first, second):
        a = jnp.sum(first, axis=0, keepdims=True)
        b = jnp.sum(second, axis=0, keepdims=True)
        half = LANES // 2
        return jnp.where(lane_row < half, a + pltpu.roll(a, half, 1), b + pltpu.roll(b, half, 1))

    curve = jnp.zeros((8, LANES), F32)
    for h in range(HALF):
        self_f[h].wait()
        forward_all(h).wait_recv()
        if h == 0:
            rim_wait(0, False)
        fold_in(h)
        to_samples()
        curve = make_stream(curve)
        if h == HALF - 1:
            sum_start(0, both(norm_part, curve))
        make_weighted()
        to_spectra()
        fold_out(h)
        if h == HALF - 1:
            sum_middle(0)
            for n in range(GROUPS):
                p, jb, g = n // 8, (n // 4) % 2, n % 4
                first, second = rolled(rim_v[0, p, jb], -KHERE * g), rolled(rim_v[1, p, jb], KHERE - KHERE * g)
                y = jnp.where(lane8 < KHERE, first, second)
                other = jnp.concatenate([y[TAPS:], y[:TAPS]], axis=0)
                back_s[n] = jnp.where(low8, y, pltpu.roll(other, LANES // 2, 1))[:TAPS]
            rim_start(rim_back)
        loop(GROUPS - 1, lambda i: backward_copy(h, i).start())
        self_b[h].start()

    sums = sum_end(0)
    zero = jnp.zeros((1, LANES), F32)
    norm_now = jnp.sum(jnp.where(lane_row < LANES // 2, sums, zero), axis=1, keepdims=True)
    alpha = norm_now / jnp.sum(jnp.where(lane_row < LANES // 2, zero, sums), axis=1, keepdims=True)

    def step_solution(i):
        part, f = i // FEEDS, lax.rem(i, FEEDS)
        nsol[part, f] = nsol[part, f] + alpha * dirv[part, f]

    loop(2 * FEEDS, step_solution)

    rim_wait(1, False)

    last8 = lax.broadcasted_iota(jnp.int32, (8, LANES), 0) >= TAPS

    def take_rim(zz):
        above = lax.rem(zz + 1, ROWS_Z) * ACROSS
        keep = jnp.where((zz == ROWS_Z - 1) & (t == SEGMENTS - 1), 0.0, 1.0).astype(F32)
        for h in range(HALF):
            for part in range(2):
                total = jnp.zeros((8, LANES), F32)
                for xx in range(ACROSS):
                    y = back_r[above + xx]
                    y = rolled(jnp.concatenate([y, y], axis=0), KHERE * (xx - h - 2 * part))
                    total = jnp.where((lane8 // KHERE == xx) & last8, y, total)
                total = total * (keep * alpha)
                y = jnp.concatenate([jnp.zeros((LANES - 8, LANES), F32), total], axis=0).T
                for xx in range(ACROSS):
                    f = HALF * xx + h
                    nres[part, f, :, frames_of(zz)] = (
                        nres[part, f, :, frames_of(zz)] - y[KHERE * xx : KHERE * (xx + 1), :]
                    )

    loop(ROWS_Z, take_rim)

    norm_next = jnp.zeros((8, LANES), F32)
    for h in range(HALF):
        self_b[h].wait()
        backward_all(h).wait_recv()

        def update(i, acc):
            part, f = i // ACROSS, HALF * lax.rem(i, ACROSS) + h
            y = nres[part, f] - alpha * recvb[part, f]
            nres[part, f] = y
            return acc + fold_rows(y * y)

        norm_next = loop(2 * ACROSS, update, norm_next)

    sum_start(1, jnp.sum(norm_next, axis=0, keepdims=True))
    sum_middle(1)
    total = jnp.sum(sum_end(1), axis=1, keepdims=True)
    beta_ref[...] = jnp.broadcast_to(total / norm_now, (8, LANES))
    for h in range(HALF):
        forward_all(h).wait_send()
        backward_all(h).wait_send()
    noise_all().wait_send()
    rim_wait(0, True)
    rim_wait(1, True)
    sum_sent(0)
    sum_sent(1)


def finish_kernel(nsol, nres, dirv, beta_ref, sol_out, res_out, dir_out, ndir, sem):
    copies = [
        pltpu.make_async_copy(nsol, sol_out, sem.at[0]),
        pltpu.make_async_copy(nres, res_out, sem.at[1]),
    ]
    for cp in copies:
        cp.start()
    beta = beta_ref[0:1, 0:1]
    for part in range(2):
        def body(f):
            ndir[part, f] = nres[part, f] + beta * dirv[part, f]

        loop(FEEDS, body)
        cp = pltpu.make_async_copy(ndir.at[part], dir_out.at[part], sem.at[2 + part])
        cp.start()
        copies.append(cp)
    for cp in copies:
        cp.wait()


def per_device(solution_, residual, direction, sample_weight):
    forward, backward = tables()
    window = window_table()
    shape = direction.shape
    vmem = pl.BlockSpec(memory_space=pltpu.VMEM)
    hbm = pl.BlockSpec(memory_space=pl.ANY)
    dma = pltpu.SemaphoreType.DMA
    piece = (2, KHERE, LANES)
    nsol, nres, dirv, beta = pl.pallas_call(
        exchange_kernel,
        name="exchange",
        out_shape=[pltpu.VMEM(shape, F32)] * 3 + [pltpu.VMEM((8, LANES), F32)],
        in_specs=[hbm] * 7,
        out_specs=[vmem] * 4,
        scratch_shapes=[
            pltpu.VMEM((HALF, GROUPS) + piece, F32),
            pltpu.VMEM((HALF, GROUPS) + piece, F32),
            pltpu.VMEM(shape, F32),
            pltpu.VMEM((ROWS_Z, ACROSS, TAPS, LANES), F32),
            pltpu.VMEM((GROUPS, TAPS, LANES), F32),
            pltpu.VMEM((GROUPS, TAPS, LANES), F32),
            pltpu.VMEM((GROUPS, TAPS, LANES), F32),
            pltpu.VMEM((HALF, QUARTER, 2, 8, LANES), F32),
            pltpu.VMEM(forward.shape, BF16),
            pltpu.VMEM(backward.shape, BF16),
            pltpu.VMEM(window.shape, F32),
            pltpu.VMEM((ACROSS, BLOCK, SAMPLES), F32),
            pltpu.VMEM((SAMPLES, LANES), F32),
            pltpu.VMEM((TILES, LANES, LANES), F32),
            pltpu.VMEM((QUARTER, 2, 2, LANES, LANES), F32),
            pltpu.VMEM((RADIX, STACK, INNER), BF16),
            pltpu.VMEM((TILES, LANES + 8, LANES), F32),
            pltpu.VMEM((TILES, LANES + 16, LANES), F32),
            pltpu.VMEM((RADIX, STACK, ROWS), BF16),
            pltpu.VMEM((RADIX, LANES + 8, INNER), F32),
            pltpu.VMEM((2, GROUPS, 1, LANES), F32),
            pltpu.VMEM((2, SEGMENTS, 1, LANES), F32),
            dma((7,)),
            dma((3, HALF)),
            dma((HALF,)),
            dma((HALF,)),
            dma((HALF,)),
            dma((HALF,)),
            dma((2,)),
            dma((2,)),
            dma((1,)),
            dma((1,)),
            dma((2,)),
            dma((2,)),
            dma((2,)),
            dma((2,)),
        ],
        compiler_params=pltpu.CompilerParams(
            collective_id=0, has_side_effects=True, vmem_limit_bytes=52 * 2**20
        ),
    )(solution_, residual, direction, sample_weight, forward, backward, window)
    inside = [pltpu.with_memory_space_constraint(x, pltpu.VMEM) for x in (nsol, nres, dirv, beta)]
    return pl.pallas_call(
        finish_kernel,
        name="finish",
        out_shape=[jax.ShapeDtypeStruct(shape, F32)] * 3,
        in_specs=[vmem] * 4,
        out_specs=[hbm] * 3,
        scratch_shapes=[pltpu.VMEM(shape, F32), dma((4,))],
        compiler_params=pltpu.CompilerParams(vmem_limit_bytes=24 * 2**20),
    )(*inside)


def solution(mesh):
    placed = P(None, None, "chan", "tm")
    return jax.shard_map(
        per_device,
        mesh=mesh,
        in_specs=(placed, placed, placed, P("tm", "chan", None, None)),
        out_specs=(placed, placed, placed),
        check_vma=False,
    )
```

```python
import math

import jax
import jax.numpy as jnp
import ml_dtypes
import numpy as np
from jax import lax
from jax.experimental import pallas as pl
from jax.experimental.pallas import tpu as pltpu
from jax.sharding import PartitionSpec as P

MESH = pl.DeviceIdType.MESH
F32 = jnp.float32
BF16 = jnp.bfloat16

SAMPLES = 2048
CHANNELS = 1024
TAPS = 4
FEEDS = 8
GROUPS = 32
SEGMENTS = 8
BLOCK = 32
KHERE = 32
HALF = 2
ACROSS = 4
LANES = ACROSS * BLOCK
TILES = SAMPLES // LANES
RIM = 16
MAIN = 2 * LANES
STACK = MAIN + 2 * RIM
RADIX = 8
ROWS = SAMPLES // RADIX
QUARTER = 4
GQ = GROUPS // QUARTER
INNER = GQ * 2 * KHERE
ROOT_HALF = math.sqrt(0.5)
PEERS = GROUPS - 1
ROWS_Z = GROUPS // ACROSS


def tables():
    j = np.arange(CHANNELS // QUARTER)
    r = np.arange(ROWS)
    s = np.arange(RADIX)
    turns = (j[None, None, :] * (RADIX * r[None, :, None] + s[:, None, None])) % SAMPLES
    angle = 2.0 * np.pi * turns / SAMPLES
    scale = 1.0 / math.sqrt(SAMPLES)
    both = np.stack([np.cos(angle) * scale, -np.sin(angle) * scale], axis=1)
    full = both.transpose(0, 1, 3, 2).reshape(RADIX, INNER, ROWS)
    high = full.astype(np.float32).astype(ml_dtypes.bfloat16)
    low = (full - high.astype(np.float64)).astype(np.float32).astype(ml_dtypes.bfloat16)
    forward = np.concatenate([high, low], axis=2)
    backward = np.concatenate([high.transpose(0, 2, 1), low.transpose(0, 2, 1)], axis=2)
    return forward, backward


def window_table():
    position = np.arange(TAPS * SAMPLES, dtype=np.float64)
    taper = 0.5 - 0.5 * np.cos(2.0 * np.pi * position / (TAPS * SAMPLES - 1))
    window = (np.sinc(position / SAMPLES - TAPS / 2) * taper).astype(np.float32)
    window = window.reshape(TAPS, ROWS, RADIX).transpose(0, 2, 1).reshape(TAPS, TILES, 1, LANES)
    return np.ascontiguousarray(np.broadcast_to(window, (TAPS, TILES, 8, LANES)))


def copy_to(src, dst, ssem, rsem, device):
    return pltpu.make_async_remote_copy(
        src_ref=src, dst_ref=dst, send_sem=ssem, recv_sem=rsem, device_id=device, device_id_type=MESH
    )


def loop(n, body, init=None):
    if init is None:
        def plain(i, carry):
            body(i)
            return carry

        lax.fori_loop(0, n, plain, 0)
        return None
    return lax.fori_loop(0, n, body, init)


def fold_rows(x):
    rows, cols = x.shape
    total = None
    for i in range(rows // 8):
        for j in range(cols // LANES):
            y = x[8 * i : 8 * i + 8, LANES * j : LANES * (j + 1)]
            total = y if total is None else total + y
    return total


def exchange_kernel(
    sol_hbm, res_hbm, dir_hbm, wgt_hbm, tf_hbm, tb_hbm, win_hbm,
    nsol, nres, dirv, beta_ref,
    recvf, sendb, recvb, rim_s, rim_r, back_s, back_r, rim_v,
    tf, tb, win, raw, nat, noise, xt, bx, sm, st, bw, vv,
    part_c, part_t,
    load_sem, self_sem, fs, fr, bs, br, rim_sent, rim_got, ns, nr, cs, cr, ts, tr,
):
    c = lax.axis_index("chan")
    t = lax.axis_index("tm")
    z, x_here = c // ACROSS, lax.rem(c, ACROSS)

    some_dev = (lax.rem(c + 1, GROUPS), t)
    t_up = lax.rem(t + 1, SEGMENTS)
    t_down = lax.rem(t + SEGMENTS - 1, SEGMENTS)
    barrier = pltpu.get_barrier_semaphore()

    def greet_chan(i):
        pl.semaphore_signal(
            barrier, inc=1, device_id=(lax.rem(c + i + 1, GROUPS), t), device_id_type=MESH
        )

    def greet_tm(i):
        pl.semaphore_signal(
            barrier, inc=1, device_id=(c, lax.rem(t + i + 1, SEGMENTS)), device_id_type=MESH
        )

    loads = [
        pltpu.make_async_copy(src, dst, load_sem.at[i])
        for i, (src, dst) in enumerate(
            (
                (dir_hbm, dirv),
                (wgt_hbm.at[0, 0], raw.at[x_here]),
                (res_hbm, nres),
                (tf_hbm, tf),
                (win_hbm, win),
                (tb_hbm, tb),
                (sol_hbm, nsol),
            )
        )
    ]
    for cp in loads:
        cp.start()
    loop(GROUPS - 1, greet_chan)
    loop(SEGMENTS - 1, greet_tm)

    def greet_up(i):
        pl.semaphore_signal(barrier, inc=1, device_id=(i, t_up), device_id_type=MESH)

    def greet_down(i):
        pl.semaphore_signal(barrier, inc=1, device_id=(i, t_down), device_id_type=MESH)

    loop(ACROSS, greet_up)

    @pl.when(z == 0)
    def _():
        loop(GROUPS, greet_down)

    def frames_of(zz):
        return pl.ds(pl.multiple_of(zz * LANES, LANES), LANES)

    def forward_copy(h, i):
        d = lax.rem(c + i + 1, GROUPS)
        src = dirv.at[:, HALF * lax.rem(d, ACROSS) + h, :, frames_of(d // ACROSS)]
        return copy_to(src, recvf.at[h, c], fs.at[h], fr.at[h], (d, t))

    def forward_all(h):
        some = recvf.at[h, pl.ds(0, GROUPS - 1)]
        return copy_to(some, some, fs.at[h], fr.at[h], some_dev)

    def spread(i):
        i = PEERS - 1 - i
        e, odd = i // 2, lax.rem(i, 2)
        return lax.rem(c + (1 + e) * (1 - odd) + (PEERS - e) * odd, GROUPS)

    def backward_copy(h, i):
        d = spread(i)
        dst = recvb.at[:, HALF * x_here + h, :, frames_of(z)]
        return copy_to(sendb.at[h, d], dst, bs.at[h], br.at[h], (d, t))

    def backward_all(h):
        some = sendb.at[h, pl.ds(0, GROUPS - 1)]
        return copy_to(some, some, bs.at[h], br.at[h], some_dev)

    def noise_copy(i):
        xx = lax.rem(x_here + i + 1, ACROSS)
        return copy_to(raw.at[x_here], raw.at[x_here], ns.at[0], nr.at[0], (z * ACROSS + xx, t))

    def noise_all():
        some = raw.at[pl.ds(0, ACROSS - 1)]
        return copy_to(some, some, ns.at[0], nr.at[0], some_dev)

    def rim_to(n):
        zz, xx = n // ACROSS, lax.rem(n, ACROSS)
        cc = lax.rem((zz + 1) * ACROSS + xx, GROUPS)
        tt = jnp.where(zz == ROWS_Z - 1, t_up, t)
        src = rim_s.at[zz, xx]
        remote = copy_to(src, rim_r.at[c], rim_sent.at[0], rim_got.at[0], (cc, tt))
        return (zz + 1) * ACROSS + xx == c, remote, pltpu.make_async_copy(src, rim_r.at[c], self_sem.at[2, 0])

    def rim_back(n):
        tt = jnp.where(z == 0, t_down, t)
        remote = copy_to(back_s.at[n], back_r.at[c], rim_sent.at[1], rim_got.at[1], (n, tt))
        own = (n == c) & (z > 0)
        return own, remote, pltpu.make_async_copy(back_s.at[n], back_r.at[c], self_sem.at[2, 1])

    def rim_start(which):
        def body(n):
            own, remote, local = which(n)

            @pl.when(own)
            def _():
                local.start()

            @pl.when(jnp.logical_not(own))
            def _():
                remote.start()

        loop(GROUPS, body)

    def rim_wait(k, sent):
        buf = rim_r if k == 0 else back_r

        def whole(n):
            some = buf.at[pl.ds(0, n)]
            cp = copy_to(some, some, rim_sent.at[k], rim_got.at[k], some_dev)
            if sent:
                cp.wait_send()
            else:
                cp.wait_recv()

        @pl.when(z == 0)
        def _():
            whole(GROUPS)

        @pl.when(z > 0)
        def _():
            whole(PEERS)
            if not sent:
                pltpu.make_async_copy(buf.at[c], buf.at[c], self_sem.at[2, k]).wait()

    here = (HALF * x_here, frames_of(z))
    self_f = [
        pltpu.make_async_copy(dirv.at[:, here[0] + h, :, here[1]], recvf.at[h, c], self_sem.at[0, h])
        for h in range(HALF)
    ]
    self_b = [
        pltpu.make_async_copy(sendb.at[h, c], recvb.at[:, here[0] + h, :, here[1]], self_sem.at[1, h])
        for h in range(HALF)
    ]

    loads[0].wait()
    for h in range(HALF):
        self_f[h].start()
    pl.semaphore_wait(barrier, PEERS + SEGMENTS - 1 + ACROSS + jnp.where(z == 0, GROUPS, 0))
    loop(GROUPS - 1, lambda i: forward_copy(0, i).start())

    low8 = lax.broadcasted_iota(jnp.int32, (8, LANES), 1) < LANES // 2

    def pack_rim(n):
        zz, fh = n // 2, lax.rem(n, 2)
        y = [
            jnp.concatenate([dirv[part, 4 * fh + f, :, frames_of(zz)] for f in range(4)], axis=0).T[LANES - 8 :]
            for part in range(2)
        ]
        rim_s[zz, 2 * fh] = jnp.where(low8, y[0], pltpu.roll(y[1], LANES // 2, 1))[TAPS:]
        rim_s[zz, 2 * fh + 1] = jnp.where(low8, pltpu.roll(y[0], LANES // 2, 1), y[1])[TAPS:]

    loop(2 * ROWS_Z, pack_rim)
    rim_start(rim_to)
    loads[1].wait()
    loop(ACROSS - 1, lambda i: noise_copy(i).start())
    loop(GROUPS - 1, lambda i: forward_copy(1, i).start())

    loads[2].wait()

    def square(i, acc):
        part, f = i // FEEDS, lax.rem(i, FEEDS)
        y = nres[part, f]
        return acc + fold_rows(y * y)

    norm_part = loop(2 * FEEDS, square, jnp.zeros((8, LANES), F32))

    noise_all().wait_recv()

    def turn(i):
        cols = pl.ds(pl.multiple_of(i * 128, 128), 128)
        nat[cols, :] = jnp.concatenate([raw[q, :, cols] for q in range(ACROSS)], axis=0).T

    loop(SAMPLES // 128, turn)
    for n in range(TILES):
        first = n // 2 + (n % 2) * (SAMPLES // 2)
        noise[n] = nat[pl.ds(first, LANES, stride=RADIX), :].T
    for cp in loads[3:]:
        cp.wait()

    keep_down = jnp.where((z == 0) & (t == 0), 0.0, 1.0).astype(F32)
    blank = jnp.zeros((8, LANES), F32)
    for n in range(TILES):
        st[n, 0:8, :] = blank
        st[n, 8 + LANES : 16 + LANES, :] = blank

    def split(x):
        high = x.astype(BF16)
        return high, (x - high.astype(F32)).astype(BF16)

    def quadrants(x):
        cols = x.shape[1] // 2

        def joined(a, b, n):
            return (x[a : a + n, :cols] + x[a : a + n, cols:]) + (x[b : b + n, :cols] + x[b : b + n, cols:])

        return joined(0, LANES, LANES), joined(MAIN, MAIN + RIM, 8)

    def rim_store(ref, s, cols, x):
        high, low = split(jnp.concatenate([x, jnp.zeros((RIM - 8, LANES), F32)], axis=0))
        ref[s, MAIN : MAIN + RIM, cols] = high
        ref[s, MAIN + RIM : STACK, cols] = low

    lane8 = lax.broadcasted_iota(jnp.int32, (8, LANES), 1)

    def rolled(x, by):
        by = by % LANES
        return pltpu.roll(x, by, 1) if by else x

    RB = 16

    def turned(re, im):
        def pairs(a, b):
            return [
                (re[a] + re[b], im[a] + im[b]),
                (re[a] - im[b], im[a] + re[b]),
                (re[a] - re[b], im[a] - im[b]),
                (re[a] + im[b], im[a] - re[b]),
            ]

        u, v = pairs(0, 2), pairs(1, 3)
        w = [
            v[0],
            ((v[1][0] - v[1][1]) * ROOT_HALF, (v[1][0] + v[1][1]) * ROOT_HALF),
            (-v[2][1], v[2][0]),
            (-(v[3][0] + v[3][1]) * ROOT_HALF, (v[3][0] - v[3][1]) * ROOT_HALF),
        ]
        return u, w

    def fold_in(h):
        def transpose(n):
            p, jb = n // 2, lax.rem(n, 2)
            for part in range(2):
                y = [recvf[h, p * GQ + jb * 4 + g, part] for g in range(4)]
                xt[p, part, jb] = jnp.concatenate(y, axis=0).T

        loop(2 * QUARTER, transpose)

        def body(n):
            jb, i = n // (LANES // RB), lax.rem(n, LANES // RB)
            rows = pl.ds(pl.multiple_of(i * RB, RB), RB)
            low_rows = pl.ds(pl.multiple_of(LANES + i * RB, RB), RB)
            re = [xt[p, 0, jb, rows, :] for p in range(QUARTER)]
            im = [xt[p, 1, jb, rows, :] for p in range(QUARTER)]

            u, w = turned(re, im)
            for s in range(4):
                for part in range(2):
                    cols = pl.ds(pl.multiple_of(part * 2 * LANES + jb * LANES, LANES), LANES)
                    for ss, y in ((s, u[s][part] + w[s][part]), (s + 4, u[s][part] - w[s][part])):
                        bx[ss, rows, cols], bx[ss, low_rows, cols] = split(y)

        loop(2 * LANES // RB, body)
        for jb in range(2):
            re, im = [], []
            for p in range(QUARTER):
                both_parts = [blank, blank]
                for g in range(4):
                    y = rim_r[p * GQ + jb * 4 + g]
                    y = jnp.concatenate([y, y], axis=0)
                    for part in range(2):
                        moved = rolled(y, KHERE * (g - h - 2 * part))
                        both_parts[part] = jnp.where(lane8 // KHERE == g, moved, both_parts[part])
                re.append(both_parts[0])
                im.append(both_parts[1])
            u, w = turned(re, im)
            for s in range(4):
                for part in range(2):
                    cols = slice((2 * part + jb) * LANES, (2 * part + jb + 1) * LANES)
                    rim_store(bx, s, cols, u[s][part] + w[s][part])
                    rim_store(bx, s + 4, cols, u[s][part] - w[s][part])

    def to_samples():
        def body(s):
            y, rim = quadrants(jnp.dot(bx[s], tf[s], preferred_element_type=F32))
            for half in range(2):
                cols = slice(half * LANES, (half + 1) * LANES)
                sm[2 * s + half, 8 : 8 + LANES, :] = y[:, cols]
                sm[2 * s + half, 8 - TAPS : 8, :] = rim[:TAPS, cols] * keep_down

        loop(RADIX, body)

    def make_stream(acc):
        def body(n, acc):
            w = [win[k, n] for k in range(TAPS)]
            for i in range(LANES // 8):
                total = w[0] * sm[n, 8 + 8 * i : 16 + 8 * i, :]
                for k in range(1, TAPS):
                    total = total + w[k] * sm[n, 8 + 8 * i - k : 16 + 8 * i - k, :]
                y = noise[n, 8 * i : 8 * i + 8, :] * total
                st[n, 8 * i + 8 : 8 * i + 16, :] = y
                acc = acc + y * total
            return acc

        return loop(TILES, body, acc)

    def make_weighted():
        def body(s):
            for half in range(2):
                n = 2 * s + half
                cols = slice(half * LANES, (half + 1) * LANES)
                w = [jnp.concatenate([win[k, n]] * (RB // 8), axis=0) for k in range(TAPS)]
                for i in range(LANES // RB):
                    total = w[0] * st[n, 8 + RB * i : 8 + RB * (i + 1), :]
                    for k in range(1, TAPS):
                        total = total + w[k] * st[n, 8 + RB * i + k : 8 + RB * (i + 1) + k, :]
                    high, low = split(total)
                    bw[s, RB * i : RB * (i + 1), cols] = high
                    bw[s, LANES + RB * i : LANES + RB * (i + 1), cols] = low
                rim = win[0, n] * st[n, 0:8, :]
                for k in range(1, TAPS):
                    rim = rim + win[k, n] * st[n, k : 8 + k, :]
                rim_store(bw, s, cols, rim)

        loop(RADIX, body)

    def to_spectra():
        def body(s):
            y, rim = quadrants(jnp.dot(bw[s], tb[s], preferred_element_type=F32))
            vv[s, :LANES, :] = y
            vv[s, LANES:, :] = rim

        loop(RADIX, body)

    def joined_image(re, im):
        ar = [re[s] + re[s + 4] for s in range(4)]
        ai = [im[s] + im[s + 4] for s in range(4)]
        dr = [re[s] - re[s + 4] for s in range(4)]
        di = [im[s] - im[s + 4] for s in range(4)]
        one = ((dr[1] + di[1]) * ROOT_HALF, (di[1] - dr[1]) * ROOT_HALF)
        one3 = ((di[1] - dr[1]) * ROOT_HALF, -(di[1] + dr[1]) * ROOT_HALF)
        three = ((di[3] - dr[3]) * ROOT_HALF, -(di[3] + dr[3]) * ROOT_HALF)
        three3 = ((dr[3] + di[3]) * ROOT_HALF, (di[3] - dr[3]) * ROOT_HALF)
        return [
            ((ar[0] + ar[2]) + (ar[1] + ar[3]), (ai[0] + ai[2]) + (ai[1] + ai[3])),
            ((dr[0] + di[2]) + (one[0] + three[0]), (di[0] - dr[2]) + (one[1] + three[1])),
            ((ar[0] - ar[2]) + (ai[1] - ai[3]), (ai[0] - ai[2]) + (ar[3] - ar[1])),
            ((dr[0] - di[2]) + (one3[0] + three3[0]), (di[0] + dr[2]) + (one3[1] + three3[1])),
        ]

    def fold_out(h):
        def body(n):
            jb, i = n // (LANES // RB), lax.rem(n, LANES // RB)
            rows = pl.ds(pl.multiple_of(i * RB, RB), RB)
            cols = [pl.ds(pl.multiple_of((2 * part + jb) * LANES, LANES), LANES) for part in range(2)]
            re = [vv[s, rows, cols[0]] for s in range(RADIX)]
            im = [vv[s, rows, cols[1]] for s in range(RADIX)]
            image = joined_image(re, im)
            for p in range(QUARTER):
                for part in range(2):
                    xt[p, part, jb, rows, :] = image[p][part]

        loop(2 * LANES // RB, body)

        for jb in range(2):
            cols = [slice((2 * part + jb) * LANES, (2 * part + jb + 1) * LANES) for part in range(2)]
            image = joined_image(*[[vv[s, LANES:, cols[part]] for s in range(RADIX)] for part in range(2)])
            for p in range(QUARTER):
                rim_v[h, p, jb] = jnp.concatenate([image[p][0][TAPS:], image[p][1][TAPS:]], axis=0)

        def transpose(n):
            p, jb = n // 2, lax.rem(n, 2)
            for part in range(2):
                y = xt[p, part, jb].T
                for g in range(4):
                    sendb[h, p * GQ + jb * 4 + g, part] = y[KHERE * g : KHERE * (g + 1), :]

        loop(2 * QUARTER, transpose)

    def tm_copy(rnd, i):
        d = lax.rem(t + i + 1, SEGMENTS)
        return copy_to(part_t.at[rnd, t], part_t.at[rnd, t], ts.at[rnd], tr.at[rnd], (c, d))

    def tm_all(rnd):
        some = part_t.at[rnd, pl.ds(0, SEGMENTS - 1)]
        return copy_to(some, some, ts.at[rnd], tr.at[rnd], some_dev)

    def chan_copy(rnd, i):
        d = lax.rem(c + i + 1, GROUPS)
        return copy_to(part_c.at[rnd, c], part_c.at[rnd, c], cs.at[rnd], cr.at[rnd], (d, t))

    def chan_all(rnd):
        some = part_c.at[rnd, pl.ds(0, GROUPS - 1)]
        return copy_to(some, some, cs.at[rnd], cr.at[rnd], some_dev)

    def sum_start(rnd, row):
        part_t[rnd, t] = row
        loop(SEGMENTS - 1, lambda i: tm_copy(rnd, i).start())

    def sum_middle(rnd):
        tm_all(rnd).wait_recv()
        part_c[rnd, c] = jnp.sum(part_t[rnd], axis=0)
        loop(GROUPS - 1, lambda i: chan_copy(rnd, i).start())

    def sum_end(rnd):
        chan_all(rnd).wait_recv()
        return jnp.sum(part_c[rnd], axis=0)

    def sum_sent(rnd):
        tm_all(rnd).wait_send()
        chan_all(rnd).wait_send()

    lane_row = lax.broadcasted_iota(jnp.int32, (1, LANES), 1)

    def both(first, second):
        a = jnp.sum(first, axis=0, keepdims=True)
        b = jnp.sum(second, axis=0, keepdims=True)
        half = LANES // 2
        return jnp.where(lane_row < half, a + pltpu.roll(a, half, 1), b + pltpu.roll(b, half, 1))

    curve = jnp.zeros((8, LANES), F32)
    for h in range(HALF):
        self_f[h].wait()
        forward_all(h).wait_recv()
        if h == 0:
            rim_wait(0, False)
        fold_in(h)
        to_samples()
        curve = make_stream(curve)
        if h == HALF - 1:
            sum_start(0, both(norm_part, curve))
        make_weighted()
        to_spectra()
        fold_out(h)
        if h == HALF - 1:
            sum_middle(0)
            for n in range(GROUPS):
                p, jb, g = n // 8, (n // 4) % 2, n % 4
                first, second = rolled(rim_v[0, p, jb], -KHERE * g), rolled(rim_v[1, p, jb], KHERE - KHERE * g)
                y = jnp.where(lane8 < KHERE, first, second)
                other = jnp.concatenate([y[TAPS:], y[:TAPS]], axis=0)
                back_s[n] = jnp.where(low8, y, pltpu.roll(other, LANES // 2, 1))[:TAPS]
            rim_start(rim_back)
        loop(GROUPS - 1, lambda i: backward_copy(h, i).start())
        self_b[h].start()

    sums = sum_end(0)
    zero = jnp.zeros((1, LANES), F32)
    norm_now = jnp.sum(jnp.where(lane_row < LANES // 2, sums, zero), axis=1, keepdims=True)
    alpha = norm_now / jnp.sum(jnp.where(lane_row < LANES // 2, zero, sums), axis=1, keepdims=True)

    def step_solution(i):
        part, f = i // FEEDS, lax.rem(i, FEEDS)
        nsol[part, f] = nsol[part, f] + alpha * dirv[part, f]

    loop(2 * FEEDS, step_solution)

    rim_wait(1, False)

    last8 = lax.broadcasted_iota(jnp.int32, (8, LANES), 0) >= TAPS

    def take_rim(zz):
        above = lax.rem(zz + 1, ROWS_Z) * ACROSS
        keep = jnp.where((zz == ROWS_Z - 1) & (t == SEGMENTS - 1), 0.0, 1.0).astype(F32)
        for h in range(HALF):
            for part in range(2):
                total = jnp.zeros((8, LANES), F32)
                for xx in range(ACROSS):
                    y = back_r[above + xx]
                    y = rolled(jnp.concatenate([y, y], axis=0), KHERE * (xx - h - 2 * part))
                    total = jnp.where((lane8 // KHERE == xx) & last8, y, total)
                total = total * (keep * alpha)
                y = jnp.concatenate([jnp.zeros((LANES - 8, LANES), F32), total], axis=0).T
                for xx in range(ACROSS):
                    f = HALF * xx + h
                    nres[part, f, :, frames_of(zz)] = (
                        nres[part, f, :, frames_of(zz)] - y[KHERE * xx : KHERE * (xx + 1), :]
                    )

    loop(ROWS_Z, take_rim)

    norm_next = jnp.zeros((8, LANES), F32)
    for h in range(HALF):
        self_b[h].wait()
        backward_all(h).wait_recv()

        def update(i, acc):
            part, f = i // ACROSS, HALF * lax.rem(i, ACROSS) + h
            y = nres[part, f] - alpha * recvb[part, f]
            nres[part, f] = y
            return acc + fold_rows(y * y)

        norm_next = loop(2 * ACROSS, update, norm_next)

    sum_start(1, jnp.sum(norm_next, axis=0, keepdims=True))
    sum_middle(1)
    total = jnp.sum(sum_end(1), axis=1, keepdims=True)
    beta_ref[...] = jnp.broadcast_to(total / norm_now, (8, LANES))
    for h in range(HALF):
        forward_all(h).wait_send()
        backward_all(h).wait_send()
    noise_all().wait_send()
    rim_wait(0, True)
    rim_wait(1, True)
    sum_sent(0)
    sum_sent(1)


def finish_kernel(nsol, nres, dirv, beta_ref, sol_out, res_out, dir_out, ndir, sem):
    copies = [
        pltpu.make_async_copy(nsol, sol_out, sem.at[0]),
        pltpu.make_async_copy(nres, res_out, sem.at[1]),
    ]
    for cp in copies:
        cp.start()
    beta = beta_ref[0:1, 0:1]
    for part in range(2):
        def body(f):
            ndir[part, f] = nres[part, f] + beta * dirv[part, f]

        loop(FEEDS, body)
        cp = pltpu.make_async_copy(ndir.at[part], dir_out.at[part], sem.at[2 + part])
        cp.start()
        copies.append(cp)
    for cp in copies:
        cp.wait()


def per_device(solution_, residual, direction, sample_weight):
    forward, backward = tables()
    window = window_table()
    shape = direction.shape
    vmem = pl.BlockSpec(memory_space=pltpu.VMEM)
    hbm = pl.BlockSpec(memory_space=pl.ANY)
    dma = pltpu.SemaphoreType.DMA
    piece = (2, KHERE, LANES)
    nsol, nres, dirv, beta = pl.pallas_call(
        exchange_kernel,
        name="exchange",
        out_shape=[pltpu.VMEM(shape, F32)] * 3 + [pltpu.VMEM((8, LANES), F32)],
        in_specs=[hbm] * 7,
        out_specs=[vmem] * 4,
        scratch_shapes=[
            pltpu.VMEM((HALF, GROUPS) + piece, F32),
            pltpu.VMEM((HALF, GROUPS) + piece, F32),
            pltpu.VMEM(shape, F32),
            pltpu.VMEM((ROWS_Z, ACROSS, TAPS, LANES), F32),
            pltpu.VMEM((GROUPS, TAPS, LANES), F32),
            pltpu.VMEM((GROUPS, TAPS, LANES), F32),
            pltpu.VMEM((GROUPS, TAPS, LANES), F32),
            pltpu.VMEM((HALF, QUARTER, 2, 8, LANES), F32),
            pltpu.VMEM(forward.shape, BF16),
            pltpu.VMEM(backward.shape, BF16),
            pltpu.VMEM(window.shape, F32),
            pltpu.VMEM((ACROSS, BLOCK, SAMPLES), F32),
            pltpu.VMEM((SAMPLES, LANES), F32),
            pltpu.VMEM((TILES, LANES, LANES), F32),
            pltpu.VMEM((QUARTER, 2, 2, LANES, LANES), F32),
            pltpu.VMEM((RADIX, STACK, INNER), BF16),
            pltpu.VMEM((TILES, LANES + 8, LANES), F32),
            pltpu.VMEM((TILES, LANES + 16, LANES), F32),
            pltpu.VMEM((RADIX, STACK, ROWS), BF16),
            pltpu.VMEM((RADIX, LANES + 8, INNER), F32),
            pltpu.VMEM((2, GROUPS, 1, LANES), F32),
            pltpu.VMEM((2, SEGMENTS, 1, LANES), F32),
            dma((7,)),
            dma((3, HALF)),
            dma((HALF,)),
            dma((HALF,)),
            dma((HALF,)),
            dma((HALF,)),
            dma((2,)),
            dma((2,)),
            dma((1,)),
            dma((1,)),
            dma((2,)),
            dma((2,)),
            dma((2,)),
            dma((2,)),
        ],
        compiler_params=pltpu.CompilerParams(
            collective_id=0, has_side_effects=True, vmem_limit_bytes=52 * 2**20
        ),
    )(solution_, residual, direction, sample_weight, forward, backward, window)
    inside = [pltpu.with_memory_space_constraint(x, pltpu.VMEM) for x in (nsol, nres, dirv, beta)]
    return pl.pallas_call(
        finish_kernel,
        name="finish",
        out_shape=[jax.ShapeDtypeStruct(shape, F32)] * 3,
        in_specs=[vmem] * 4,
        out_specs=[hbm] * 3,
        scratch_shapes=[pltpu.VMEM(shape, F32), dma((4,))],
        compiler_params=pltpu.CompilerParams(vmem_limit_bytes=24 * 2**20),
    )(*inside)


def solution(mesh):
    placed = P(None, None, "chan", "tm")
    return jax.shard_map(
        per_device,
        mesh=mesh,
        in_specs=(placed, placed, placed, P("tm", "chan", None, None)),
        out_specs=(placed, placed, placed),
        check_vma=False,
    )
```

```python
import math

import jax
import jax.numpy as jnp
import ml_dtypes
import numpy as np
from jax import lax
from jax.experimental import pallas as pl
from jax.experimental.pallas import tpu as pltpu
from jax.sharding import PartitionSpec as P

MESH = pl.DeviceIdType.MESH
F32 = jnp.float32
BF16 = jnp.bfloat16

SAMPLES = 2048
CHANNELS = 1024
TAPS = 4
FEEDS = 8
GROUPS = 32
SEGMENTS = 8
BLOCK = 32
KHERE = 32
HALF = 2
ACROSS = 4
LANES = ACROSS * BLOCK
TILES = SAMPLES // LANES
RIM = 16
MAIN = 2 * LANES
STACK = MAIN + 2 * RIM
RADIX = 8
ROWS = SAMPLES // RADIX
QUARTER = 4
GQ = GROUPS // QUARTER
INNER = GQ * 2 * KHERE
ROOT_HALF = math.sqrt(0.5)
PEERS = GROUPS - 1
ROWS_Z = GROUPS // ACROSS


def tables():
    j = np.arange(CHANNELS // QUARTER)
    r = np.arange(ROWS)
    s = np.arange(RADIX)
    turns = (j[None, None, :] * (RADIX * r[None, :, None] + s[:, None, None])) % SAMPLES
    angle = 2.0 * np.pi * turns / SAMPLES
    scale = 1.0 / math.sqrt(SAMPLES)
    both = np.stack([np.cos(angle) * scale, -np.sin(angle) * scale], axis=1)
    full = both.transpose(0, 1, 3, 2).reshape(RADIX, INNER, ROWS)
    high = full.astype(np.float32).astype(ml_dtypes.bfloat16)
    low = (full - high.astype(np.float64)).astype(np.float32).astype(ml_dtypes.bfloat16)
    forward = np.concatenate([high, low], axis=2)
    backward = np.concatenate([high.transpose(0, 2, 1), low.transpose(0, 2, 1)], axis=2)
    return forward, backward


def window_table():
    position = np.arange(TAPS * SAMPLES, dtype=np.float64)
    taper = 0.5 - 0.5 * np.cos(2.0 * np.pi * position / (TAPS * SAMPLES - 1))
    window = (np.sinc(position / SAMPLES - TAPS / 2) * taper).astype(np.float32)
    window = window.reshape(TAPS, ROWS, RADIX).transpose(0, 2, 1).reshape(TAPS, TILES, 1, LANES)
    return np.ascontiguousarray(np.broadcast_to(window, (TAPS, TILES, 8, LANES)))


def copy_to(src, dst, ssem, rsem, device):
    return pltpu.make_async_remote_copy(
        src_ref=src, dst_ref=dst, send_sem=ssem, recv_sem=rsem, device_id=device, device_id_type=MESH
    )


def loop(n, body, init=None):
    if init is None:
        def plain(i, carry):
            body(i)
            return carry

        lax.fori_loop(0, n, plain, 0)
        return None
    return lax.fori_loop(0, n, body, init)


def fold_rows(x):
    rows, cols = x.shape
    total = None
    for i in range(rows // 8):
        for j in range(cols // LANES):
            y = x[8 * i : 8 * i + 8, LANES * j : LANES * (j + 1)]
            total = y if total is None else total + y
    return total


def exchange_kernel(
    sol_hbm, res_hbm, dir_hbm, wgt_hbm, tf_hbm, tb_hbm, win_hbm,
    nsol, nres, dirv, beta_ref,
    recvf, sendb, recvb, rim_s, rim_r, back_s, back_r, rim_v,
    tf, tb, win, raw, nat, noise, xt, bx, sm, st, bw, vv,
    part_c, part_t,
    load_sem, self_sem, fs, fr, bs, br, rim_sent, rim_got, ns, nr, cs, cr, ts, tr,
):
    c = lax.axis_index("chan")
    t = lax.axis_index("tm")
    z, x_here = c // ACROSS, lax.rem(c, ACROSS)

    some_dev = (lax.rem(c + 1, GROUPS), t)
    t_up = lax.rem(t + 1, SEGMENTS)
    t_down = lax.rem(t + SEGMENTS - 1, SEGMENTS)
    barrier = pltpu.get_barrier_semaphore()

    def greet_chan(i):
        pl.semaphore_signal(
            barrier, inc=1, device_id=(lax.rem(c + i + 1, GROUPS), t), device_id_type=MESH
        )

    def greet_tm(i):
        pl.semaphore_signal(
            barrier, inc=1, device_id=(c, lax.rem(t + i + 1, SEGMENTS)), device_id_type=MESH
        )

    loads = [
        pltpu.make_async_copy(src, dst, load_sem.at[i])
        for i, (src, dst) in enumerate(
            (
                (dir_hbm, dirv),
                (wgt_hbm.at[0, 0], raw.at[x_here]),
                (res_hbm, nres),
                (tf_hbm, tf),
                (win_hbm, win),
                (tb_hbm, tb),
                (sol_hbm, nsol),
            )
        )
    ]
    for cp in loads[:2]:
        cp.start()
    loop(GROUPS - 1, greet_chan)
    loop(SEGMENTS - 1, greet_tm)

    def greet_up(i):
        pl.semaphore_signal(barrier, inc=1, device_id=(i, t_up), device_id_type=MESH)

    def greet_down(i):
        pl.semaphore_signal(barrier, inc=1, device_id=(i, t_down), device_id_type=MESH)

    loop(ACROSS, greet_up)

    @pl.when(z == 0)
    def _():
        loop(GROUPS, greet_down)

    def frames_of(zz):
        return pl.ds(pl.multiple_of(zz * LANES, LANES), LANES)

    def forward_copy(h, i):
        d = lax.rem(c + i + 1, GROUPS)
        src = dirv.at[:, HALF * lax.rem(d, ACROSS) + h, :, frames_of(d // ACROSS)]
        return copy_to(src, recvf.at[h, c], fs.at[h], fr.at[h], (d, t))

    def forward_all(h):
        some = recvf.at[h, pl.ds(0, GROUPS - 1)]
        return copy_to(some, some, fs.at[h], fr.at[h], some_dev)

    def spread(i):
        i = PEERS - 1 - i
        e, odd = i // 2, lax.rem(i, 2)
        return lax.rem(c + (1 + e) * (1 - odd) + (PEERS - e) * odd, GROUPS)

    def backward_copy(h, i):
        d = spread(i)
        dst = recvb.at[:, HALF * x_here + h, :, frames_of(z)]
        return copy_to(sendb.at[h, d], dst, bs.at[h], br.at[h], (d, t))

    def backward_all(h):
        some = sendb.at[h, pl.ds(0, GROUPS - 1)]
        return copy_to(some, some, bs.at[h], br.at[h], some_dev)

    def noise_copy(i):
        xx = lax.rem(x_here + i + 1, ACROSS)
        return copy_to(raw.at[x_here], raw.at[x_here], ns.at[0], nr.at[0], (z * ACROSS + xx, t))

    def noise_all():
        some = raw.at[pl.ds(0, ACROSS - 1)]
        return copy_to(some, some, ns.at[0], nr.at[0], some_dev)

    def rim_to(n):
        zz, xx = n // ACROSS, lax.rem(n, ACROSS)
        cc = lax.rem((zz + 1) * ACROSS + xx, GROUPS)
        tt = jnp.where(zz == ROWS_Z - 1, t_up, t)
        src = rim_s.at[zz, xx]
        remote = copy_to(src, rim_r.at[c], rim_sent.at[0], rim_got.at[0], (cc, tt))
        return (zz + 1) * ACROSS + xx == c, remote, pltpu.make_async_copy(src, rim_r.at[c], self_sem.at[2, 0])

    def rim_back(n):
        tt = jnp.where(z == 0, t_down, t)
        remote = copy_to(back_s.at[n], back_r.at[c], rim_sent.at[1], rim_got.at[1], (n, tt))
        own = (n == c) & (z > 0)
        return own, remote, pltpu.make_async_copy(back_s.at[n], back_r.at[c], self_sem.at[2, 1])

    def rim_start(which):
        def body(n):
            own, remote, local = which(n)

            @pl.when(own)
            def _():
                local.start()

            @pl.when(jnp.logical_not(own))
            def _():
                remote.start()

        loop(GROUPS, body)

    def rim_wait(k, sent):
        buf = rim_r if k == 0 else back_r

        def whole(n):
            some = buf.at[pl.ds(0, n)]
            cp = copy_to(some, some, rim_sent.at[k], rim_got.at[k], some_dev)
            if sent:
                cp.wait_send()
            else:
                cp.wait_recv()

        @pl.when(z == 0)
        def _():
            whole(GROUPS)

        @pl.when(z > 0)
        def _():
            whole(PEERS)
            if not sent:
                pltpu.make_async_copy(buf.at[c], buf.at[c], self_sem.at[2, k]).wait()

    here = (HALF * x_here, frames_of(z))
    self_f = [
        pltpu.make_async_copy(dirv.at[:, here[0] + h, :, here[1]], recvf.at[h, c], self_sem.at[0, h])
        for h in range(HALF)
    ]
    self_b = [
        pltpu.make_async_copy(sendb.at[h, c], recvb.at[:, here[0] + h, :, here[1]], self_sem.at[1, h])
        for h in range(HALF)
    ]

    loads[0].wait()
    for h in range(HALF):
        self_f[h].start()
    pl.semaphore_wait(barrier, PEERS + SEGMENTS - 1 + ACROSS + jnp.where(z == 0, GROUPS, 0))
    loop(GROUPS - 1, lambda i: forward_copy(0, i).start())
    for cp in loads[2:]:
        cp.start()

    low8 = lax.broadcasted_iota(jnp.int32, (8, LANES), 1) < LANES // 2

    def pack_rim(n):
        zz, fh = n // 2, lax.rem(n, 2)
        y = [
            jnp.concatenate([dirv[part, 4 * fh + f, :, frames_of(zz)] for f in range(4)], axis=0).T[LANES - 8 :]
            for part in range(2)
        ]
        rim_s[zz, 2 * fh] = jnp.where(low8, y[0], pltpu.roll(y[1], LANES // 2, 1))[TAPS:]
        rim_s[zz, 2 * fh + 1] = jnp.where(low8, pltpu.roll(y[0], LANES // 2, 1), y[1])[TAPS:]

    loop(2 * ROWS_Z, pack_rim)
    rim_start(rim_to)
    loads[1].wait()
    loop(ACROSS - 1, lambda i: noise_copy(i).start())
    loop(GROUPS - 1, lambda i: forward_copy(1, i).start())

    loads[2].wait()

    def square(i, acc):
        part, f = i // FEEDS, lax.rem(i, FEEDS)
        y = nres[part, f]
        return acc + fold_rows(y * y)

    norm_part = loop(2 * FEEDS, square, jnp.zeros((8, LANES), F32))

    noise_all().wait_recv()

    def turn(i):
        cols = pl.ds(pl.multiple_of(i * 128, 128), 128)
        nat[cols, :] = jnp.concatenate([raw[q, :, cols] for q in range(ACROSS)], axis=0).T

    loop(SAMPLES // 128, turn)
    for n in range(TILES):
        first = n // 2 + (n % 2) * (SAMPLES // 2)
        noise[n] = nat[pl.ds(first, LANES, stride=RADIX), :].T
    for cp in loads[3:]:
        cp.wait()

    keep_down = jnp.where((z == 0) & (t == 0), 0.0, 1.0).astype(F32)
    blank = jnp.zeros((8, LANES), F32)
    for n in range(TILES):
        st[n, 0:8, :] = blank
        st[n, 8 + LANES : 16 + LANES, :] = blank

    def split(x):
        high = x.astype(BF16)
        return high, (x - high.astype(F32)).astype(BF16)

    def quadrants(x):
        cols = x.shape[1] // 2

        def joined(a, b, n):
            return (x[a : a + n, :cols] + x[a : a + n, cols:]) + (x[b : b + n, :cols] + x[b : b + n, cols:])

        return joined(0, LANES, LANES), joined(MAIN, MAIN + RIM, 8)

    def rim_store(ref, s, cols, x):
        high, low = split(jnp.concatenate([x, jnp.zeros((RIM - 8, LANES), F32)], axis=0))
        ref[s, MAIN : MAIN + RIM, cols] = high
        ref[s, MAIN + RIM : STACK, cols] = low

    lane8 = lax.broadcasted_iota(jnp.int32, (8, LANES), 1)

    def rolled(x, by):
        by = by % LANES
        return pltpu.roll(x, by, 1) if by else x

    RB = 16

    def turned(re, im):
        def pairs(a, b):
            return [
                (re[a] + re[b], im[a] + im[b]),
                (re[a] - im[b], im[a] + re[b]),
                (re[a] - re[b], im[a] - im[b]),
                (re[a] + im[b], im[a] - re[b]),
            ]

        u, v = pairs(0, 2), pairs(1, 3)
        w = [
            v[0],
            ((v[1][0] - v[1][1]) * ROOT_HALF, (v[1][0] + v[1][1]) * ROOT_HALF),
            (-v[2][1], v[2][0]),
            (-(v[3][0] + v[3][1]) * ROOT_HALF, (v[3][0] - v[3][1]) * ROOT_HALF),
        ]
        return u, w

    def fold_in(h):
        def transpose(n):
            p, jb = n // 2, lax.rem(n, 2)
            for part in range(2):
                y = [recvf[h, p * GQ + jb * 4 + g, part] for g in range(4)]
                xt[p, part, jb] = jnp.concatenate(y, axis=0).T

        loop(2 * QUARTER, transpose)

        def body(n):
            jb, i = n // (LANES // RB), lax.rem(n, LANES // RB)
            rows = pl.ds(pl.multiple_of(i * RB, RB), RB)
            low_rows = pl.ds(pl.multiple_of(LANES + i * RB, RB), RB)
            re = [xt[p, 0, jb, rows, :] for p in range(QUARTER)]
            im = [xt[p, 1, jb, rows, :] for p in range(QUARTER)]

            u, w = turned(re, im)
            for s in range(4):
                for part in range(2):
                    cols = pl.ds(pl.multiple_of(part * 2 * LANES + jb * LANES, LANES), LANES)
                    for ss, y in ((s, u[s][part] + w[s][part]), (s + 4, u[s][part] - w[s][part])):
                        bx[ss, rows, cols], bx[ss, low_rows, cols] = split(y)

        loop(2 * LANES // RB, body)
        for jb in range(2):
            re, im = [], []
            for p in range(QUARTER):
                both_parts = [blank, blank]
                for g in range(4):
                    y = rim_r[p * GQ + jb * 4 + g]
                    y = jnp.concatenate([y, y], axis=0)
                    for part in range(2):
                        moved = rolled(y, KHERE * (g - h - 2 * part))
                        both_parts[part] = jnp.where(lane8 // KHERE == g, moved, both_parts[part])
                re.append(both_parts[0])
                im.append(both_parts[1])
            u, w = turned(re, im)
            for s in range(4):
                for part in range(2):
                    cols = slice((2 * part + jb) * LANES, (2 * part + jb + 1) * LANES)
                    rim_store(bx, s, cols, u[s][part] + w[s][part])
                    rim_store(bx, s + 4, cols, u[s][part] - w[s][part])

    def to_samples():
        def body(s):
            y, rim = quadrants(jnp.dot(bx[s], tf[s], preferred_element_type=F32))
            for half in range(2):
                cols = slice(half * LANES, (half + 1) * LANES)
                sm[2 * s + half, 8 : 8 + LANES, :] = y[:, cols]
                sm[2 * s + half, 8 - TAPS : 8, :] = rim[:TAPS, cols] * keep_down

        loop(RADIX, body)

    def make_stream(acc):
        def body(n, acc):
            w = [win[k, n] for k in range(TAPS)]
            for i in range(LANES // 8):
                total = w[0] * sm[n, 8 + 8 * i : 16 + 8 * i, :]
                for k in range(1, TAPS):
                    total = total + w[k] * sm[n, 8 + 8 * i - k : 16 + 8 * i - k, :]
                y = noise[n, 8 * i : 8 * i + 8, :] * total
                st[n, 8 * i + 8 : 8 * i + 16, :] = y
                acc = acc + y * total
            return acc

        return loop(TILES, body, acc)

    def make_weighted():
        def body(s):
            for half in range(2):
                n = 2 * s + half
                cols = slice(half * LANES, (half + 1) * LANES)
                w = [jnp.concatenate([win[k, n]] * (RB // 8), axis=0) for k in range(TAPS)]
                for i in range(LANES // RB):
                    total = w[0] * st[n, 8 + RB * i : 8 + RB * (i + 1), :]
                    for k in range(1, TAPS):
                        total = total + w[k] * st[n, 8 + RB * i + k : 8 + RB * (i + 1) + k, :]
                    high, low = split(total)
                    bw[s, RB * i : RB * (i + 1), cols] = high
                    bw[s, LANES + RB * i : LANES + RB * (i + 1), cols] = low
                rim = win[0, n] * st[n, 0:8, :]
                for k in range(1, TAPS):
                    rim = rim + win[k, n] * st[n, k : 8 + k, :]
                rim_store(bw, s, cols, rim)

        loop(RADIX, body)

    def to_spectra():
        def body(s):
            y, rim = quadrants(jnp.dot(bw[s], tb[s], preferred_element_type=F32))
            vv[s, :LANES, :] = y
            vv[s, LANES:, :] = rim

        loop(RADIX, body)

    def joined_image(re, im):
        ar = [re[s] + re[s + 4] for s in range(4)]
        ai = [im[s] + im[s + 4] for s in range(4)]
        dr = [re[s] - re[s + 4] for s in range(4)]
        di = [im[s] - im[s + 4] for s in range(4)]
        one = ((dr[1] + di[1]) * ROOT_HALF, (di[1] - dr[1]) * ROOT_HALF)
        one3 = ((di[1] - dr[1]) * ROOT_HALF, -(di[1] + dr[1]) * ROOT_HALF)
        three = ((di[3] - dr[3]) * ROOT_HALF, -(di[3] + dr[3]) * ROOT_HALF)
        three3 = ((dr[3] + di[3]) * ROOT_HALF, (di[3] - dr[3]) * ROOT_HALF)
        return [
            ((ar[0] + ar[2]) + (ar[1] + ar[3]), (ai[0] + ai[2]) + (ai[1] + ai[3])),
            ((dr[0] + di[2]) + (one[0] + three[0]), (di[0] - dr[2]) + (one[1] + three[1])),
            ((ar[0] - ar[2]) + (ai[1] - ai[3]), (ai[0] - ai[2]) + (ar[3] - ar[1])),
            ((dr[0] - di[2]) + (one3[0] + three3[0]), (di[0] + dr[2]) + (one3[1] + three3[1])),
        ]

    def fold_out(h):
        def body(n):
            jb, i = n // (LANES // RB), lax.rem(n, LANES // RB)
            rows = pl.ds(pl.multiple_of(i * RB, RB), RB)
            cols = [pl.ds(pl.multiple_of((2 * part + jb) * LANES, LANES), LANES) for part in range(2)]
            re = [vv[s, rows, cols[0]] for s in range(RADIX)]
            im = [vv[s, rows, cols[1]] for s in range(RADIX)]
            image = joined_image(re, im)
            for p in range(QUARTER):
                for part in range(2):
                    xt[p, part, jb, rows, :] = image[p][part]

        loop(2 * LANES // RB, body)

        for jb in range(2):
            cols = [slice((2 * part + jb) * LANES, (2 * part + jb + 1) * LANES) for part in range(2)]
            image = joined_image(*[[vv[s, LANES:, cols[part]] for s in range(RADIX)] for part in range(2)])
            for p in range(QUARTER):
                rim_v[h, p, jb] = jnp.concatenate([image[p][0][TAPS:], image[p][1][TAPS:]], axis=0)

        def transpose(n):
            p, jb = n // 2, lax.rem(n, 2)
            for part in range(2):
                y = xt[p, part, jb].T
                for g in range(4):
                    sendb[h, p * GQ + jb * 4 + g, part] = y[KHERE * g : KHERE * (g + 1), :]

        loop(2 * QUARTER, transpose)

    def tm_copy(rnd, i):
        d = lax.rem(t + i + 1, SEGMENTS)
        return copy_to(part_t.at[rnd, t], part_t.at[rnd, t], ts.at[rnd], tr.at[rnd], (c, d))

    def tm_all(rnd):
        some = part_t.at[rnd, pl.ds(0, SEGMENTS - 1)]
        return copy_to(some, some, ts.at[rnd], tr.at[rnd], some_dev)

    def chan_copy(rnd, i):
        d = lax.rem(c + i + 1, GROUPS)
        return copy_to(part_c.at[rnd, c], part_c.at[rnd, c], cs.at[rnd], cr.at[rnd], (d, t))

    def chan_all(rnd):
        some = part_c.at[rnd, pl.ds(0, GROUPS - 1)]
        return copy_to(some, some, cs.at[rnd], cr.at[rnd], some_dev)

    def sum_start(rnd, row):
        part_t[rnd, t] = row
        loop(SEGMENTS - 1, lambda i: tm_copy(rnd, i).start())

    def sum_middle(rnd):
        tm_all(rnd).wait_recv()
        part_c[rnd, c] = jnp.sum(part_t[rnd], axis=0)
        loop(GROUPS - 1, lambda i: chan_copy(rnd, i).start())

    def sum_end(rnd):
        chan_all(rnd).wait_recv()
        return jnp.sum(part_c[rnd], axis=0)

    def sum_sent(rnd):
        tm_all(rnd).wait_send()
        chan_all(rnd).wait_send()

    lane_row = lax.broadcasted_iota(jnp.int32, (1, LANES), 1)

    def both(first, second):
        a = jnp.sum(first, axis=0, keepdims=True)
        b = jnp.sum(second, axis=0, keepdims=True)
        half = LANES // 2
        return jnp.where(lane_row < half, a + pltpu.roll(a, half, 1), b + pltpu.roll(b, half, 1))

    curve = jnp.zeros((8, LANES), F32)
    for h in range(HALF):
        self_f[h].wait()
        forward_all(h).wait_recv()
        if h == 0:
            rim_wait(0, False)
        fold_in(h)
        to_samples()
        curve = make_stream(curve)
        if h == HALF - 1:
            sum_start(0, both(norm_part, curve))
        make_weighted()
        to_spectra()
        fold_out(h)
        if h == HALF - 1:
            sum_middle(0)
            for n in range(GROUPS):
                p, jb, g = n // 8, (n // 4) % 2, n % 4
                first, second = rolled(rim_v[0, p, jb], -KHERE * g), rolled(rim_v[1, p, jb], KHERE - KHERE * g)
                y = jnp.where(lane8 < KHERE, first, second)
                other = jnp.concatenate([y[TAPS:], y[:TAPS]], axis=0)
                back_s[n] = jnp.where(low8, y, pltpu.roll(other, LANES // 2, 1))[:TAPS]
            rim_start(rim_back)
        loop(GROUPS - 1, lambda i: backward_copy(h, i).start())
        self_b[h].start()

    sums = sum_end(0)
    zero = jnp.zeros((1, LANES), F32)
    norm_now = jnp.sum(jnp.where(lane_row < LANES // 2, sums, zero), axis=1, keepdims=True)
    alpha = norm_now / jnp.sum(jnp.where(lane_row < LANES // 2, zero, sums), axis=1, keepdims=True)

    def step_solution(i):
        part, f = i // FEEDS, lax.rem(i, FEEDS)
        nsol[part, f] = nsol[part, f] + alpha * dirv[part, f]

    loop(2 * FEEDS, step_solution)

    rim_wait(1, False)

    last8 = lax.broadcasted_iota(jnp.int32, (8, LANES), 0) >= TAPS

    def take_rim(zz):
        above = lax.rem(zz + 1, ROWS_Z) * ACROSS
        keep = jnp.where((zz == ROWS_Z - 1) & (t == SEGMENTS - 1), 0.0, 1.0).astype(F32)
        for h in range(HALF):
            for part in range(2):
                total = jnp.zeros((8, LANES), F32)
                for xx in range(ACROSS):
                    y = back_r[above + xx]
                    y = rolled(jnp.concatenate([y, y], axis=0), KHERE * (xx - h - 2 * part))
                    total = jnp.where((lane8 // KHERE == xx) & last8, y, total)
                total = total * (keep * alpha)
                y = jnp.concatenate([jnp.zeros((LANES - 8, LANES), F32), total], axis=0).T
                for xx in range(ACROSS):
                    f = HALF * xx + h
                    nres[part, f, :, frames_of(zz)] = (
                        nres[part, f, :, frames_of(zz)] - y[KHERE * xx : KHERE * (xx + 1), :]
                    )

    loop(ROWS_Z, take_rim)

    norm_next = jnp.zeros((8, LANES), F32)
    for h in range(HALF):
        self_b[h].wait()
        backward_all(h).wait_recv()

        def update(i, acc):
            part, f = i // ACROSS, HALF * lax.rem(i, ACROSS) + h
            y = nres[part, f] - alpha * recvb[part, f]
            nres[part, f] = y
            return acc + fold_rows(y * y)

        norm_next = loop(2 * ACROSS, update, norm_next)

    sum_start(1, jnp.sum(norm_next, axis=0, keepdims=True))
    sum_middle(1)
    total = jnp.sum(sum_end(1), axis=1, keepdims=True)
    beta_ref[...] = jnp.broadcast_to(total / norm_now, (8, LANES))
    for h in range(HALF):
        forward_all(h).wait_send()
        backward_all(h).wait_send()
    noise_all().wait_send()
    rim_wait(0, True)
    rim_wait(1, True)
    sum_sent(0)
    sum_sent(1)


def finish_kernel(nsol, nres, dirv, beta_ref, sol_out, res_out, dir_out, ndir, sem):
    copies = [
        pltpu.make_async_copy(nsol, sol_out, sem.at[0]),
        pltpu.make_async_copy(nres, res_out, sem.at[1]),
    ]
    for cp in copies:
        cp.start()
    beta = beta_ref[0:1, 0:1]
    for part in range(2):
        def body(f):
            ndir[part, f] = nres[part, f] + beta * dirv[part, f]

        loop(FEEDS, body)
        cp = pltpu.make_async_copy(ndir.at[part], dir_out.at[part], sem.at[2 + part])
        cp.start()
        copies.append(cp)
    for cp in copies:
        cp.wait()


def per_device(solution_, residual, direction, sample_weight):
    forward, backward = tables()
    window = window_table()
    shape = direction.shape
    vmem = pl.BlockSpec(memory_space=pltpu.VMEM)
    hbm = pl.BlockSpec(memory_space=pl.ANY)
    dma = pltpu.SemaphoreType.DMA
    piece = (2, KHERE, LANES)
    nsol, nres, dirv, beta = pl.pallas_call(
        exchange_kernel,
        name="exchange",
        out_shape=[pltpu.VMEM(shape, F32)] * 3 + [pltpu.VMEM((8, LANES), F32)],
        in_specs=[hbm] * 7,
        out_specs=[vmem] * 4,
        scratch_shapes=[
            pltpu.VMEM((HALF, GROUPS) + piece, F32),
            pltpu.VMEM((HALF, GROUPS) + piece, F32),
            pltpu.VMEM(shape, F32),
            pltpu.VMEM((ROWS_Z, ACROSS, TAPS, LANES), F32),
            pltpu.VMEM((GROUPS, TAPS, LANES), F32),
            pltpu.VMEM((GROUPS, TAPS, LANES), F32),
            pltpu.VMEM((GROUPS, TAPS, LANES), F32),
            pltpu.VMEM((HALF, QUARTER, 2, 8, LANES), F32),
            pltpu.VMEM(forward.shape, BF16),
            pltpu.VMEM(backward.shape, BF16),
            pltpu.VMEM(window.shape, F32),
            pltpu.VMEM((ACROSS, BLOCK, SAMPLES), F32),
            pltpu.VMEM((SAMPLES, LANES), F32),
            pltpu.VMEM((TILES, LANES, LANES), F32),
            pltpu.VMEM((QUARTER, 2, 2, LANES, LANES), F32),
            pltpu.VMEM((RADIX, STACK, INNER), BF16),
            pltpu.VMEM((TILES, LANES + 8, LANES), F32),
            pltpu.VMEM((TILES, LANES + 16, LANES), F32),
            pltpu.VMEM((RADIX, STACK, ROWS), BF16),
            pltpu.VMEM((RADIX, LANES + 8, INNER), F32),
            pltpu.VMEM((2, GROUPS, 1, LANES), F32),
            pltpu.VMEM((2, SEGMENTS, 1, LANES), F32),
            dma((7,)),
            dma((3, HALF)),
            dma((HALF,)),
            dma((HALF,)),
            dma((HALF,)),
            dma((HALF,)),
            dma((2,)),
            dma((2,)),
            dma((1,)),
            dma((1,)),
            dma((2,)),
            dma((2,)),
            dma((2,)),
            dma((2,)),
        ],
        compiler_params=pltpu.CompilerParams(
            collective_id=0, has_side_effects=True, vmem_limit_bytes=52 * 2**20
        ),
    )(solution_, residual, direction, sample_weight, forward, backward, window)
    inside = [pltpu.with_memory_space_constraint(x, pltpu.VMEM) for x in (nsol, nres, dirv, beta)]
    return pl.pallas_call(
        finish_kernel,
        name="finish",
        out_shape=[jax.ShapeDtypeStruct(shape, F32)] * 3,
        in_specs=[vmem] * 4,
        out_specs=[hbm] * 3,
        scratch_shapes=[pltpu.VMEM(shape, F32), dma((4,))],
        compiler_params=pltpu.CompilerParams(vmem_limit_bytes=24 * 2**20),
    )(*inside)


def solution(mesh):
    placed = P(None, None, "chan", "tm")
    return jax.shard_map(
        per_device,
        mesh=mesh,
        in_specs=(placed, placed, placed, P("tm", "chan", None, None)),
        out_specs=(placed, placed, placed),
        check_vma=False,
    )
```
